256 devices in a mesh: gz: 32 (over x_lo, z, core), box: 8 (over x_hi, y).
Axes of the slice: x: 4 (x_hi: 2, x_lo: 2; x = x_hi * 2 + x_lo), y: 4, z: 8, core: 2. Of those that a mesh axis runs over, the one named last changes fastest.
Arguments:
- sources: float32 [512, 16, 16, 1024], P('gz', 'box'), may hold values from -6 to 6
- leaf_maps: float32 [32, 16, 1024, 1024], P('gz', 'box'), may hold values from -1 to 1, as said below
- mode_ids: int32 [32], replicated, may hold values from 0 to 511, as said below
Outputs:
- merged_map: float32 [32, 8, 512, 1024], P('gz', 'box')
- merged_data: float32 [32, 8, 16, 512], P('gz', 'box')
The draws below stay inside these ranges and needn't reach their ends.
Inputs may be any that keep to these rules, and one draw needn't show every extreme that they name: `mode_ids`: distinct mode numbers; 0 and 511 are always among them. `leaf_maps`: every leaf map is a contraction: its operator norm is below 1.
All inputs are finite; a program needn't handle non-finite values.
Results may differ from the reference program's by a relative error of at most 0.000082.
Values sent between devices are 32-bit elements; how exact they have to be, the bound alone decides.
A program may use at most 128 MiB of HBM per device.

```python
import jax
import jax.numpy as jnp
from jax import lax

NB = 1024
NZ = 512
NRHS = 16
NP = 512
MODES = 32
BOXES = 16


def cosine_table(freq_index, point_index, face):
    phase = (2 * point_index + 1) * freq_index % (4 * face)
    angle = phase.astype(jnp.float32) * (jnp.pi / (2.0 * face))
    weight = jnp.where(freq_index == 0, (1.0 / face) ** 0.5, (2.0 / face) ** 0.5)
    return weight * jnp.cos(angle)


def one_leaf(key):
    keys = jax.random.split(key, 9)
    row_perm = jnp.concatenate([jax.random.permutation(keys[0], NP), jax.random.permutation(keys[1], NP)]).astype(jnp.int32)
    col_perm = jnp.concatenate([jax.random.permutation(keys[2], NP), jax.random.permutation(keys[3], NP)]).astype(jnp.int32)
    row_sign = jnp.where(jax.random.bernoulli(keys[4], 0.5, (NB,)), 1.0, -1.0).astype(jnp.float32)
    col_sign = jnp.where(jax.random.bernoulli(keys[5], 0.5, (NB,)), 1.0, -1.0).astype(jnp.float32)
    noise_std = 0.05 / (2.0 * NB ** 0.5)
    scale_c = jax.random.uniform(keys[6], (), jnp.float32, 0.85, 0.92)
    cos_t = jax.random.uniform(keys[7], (), jnp.float32, 0.8, 0.95)
    noise = jnp.clip(jax.random.normal(keys[8], (NB, NB), jnp.float32), -4.0, 4.0) * noise_std
    sin_t = jnp.sqrt(1.0 - cos_t * cos_t)
    face_of = (jnp.arange(NB, dtype=jnp.int32) >= NP).astype(jnp.int32)
    row_face = face_of[:, None]
    col_face = face_of[None, :]
    rotation = jnp.where(row_face == col_face, cos_t, jnp.where(row_face < col_face, sin_t, -sin_t))
    table = cosine_table(row_perm[:, None], col_perm[None, :], NP)
    return (scale_c * row_sign[:, None] * col_sign[None, :] * rotation * table + noise).astype(jnp.float32)


def draw_leaf_maps(key, part):

    def per_mode(mode_index):
        mode_key = jax.random.fold_in(jax.random.fold_in(key, 101), mode_index)
        box_keys = jax.vmap(lambda box_index: jax.random.fold_in(mode_key, box_index))(jnp.arange(BOXES, dtype=jnp.int32))
        return jax.vmap(one_leaf)(box_keys)
    values = lax.map(per_mode, jnp.arange(MODES, dtype=jnp.int32))
    return values.astype(jnp.float32)


def draw_mode_ids(key, part):
    inner = jax.random.permutation(key, NZ - 2)[:MODES - 2].astype(jnp.int32) + 1
    ends = jnp.array([0, NZ - 1], dtype=jnp.int32)
    joined = jnp.concatenate([ends, inner])
    order = jax.random.permutation(jax.random.fold_in(key, 7), MODES)
    return joined[order].astype(jnp.int32)


def levels(rng, dims, cuts, smallest, largest):
    level, own = 1.0, jax.random.fold_in(rng, 6)
    for position, parts in cuts:
        steps = jnp.exp(jax.random.uniform(jax.random.fold_in(own, position), (parts,), jnp.float32, smallest / len(cuts), largest / len(cuts)))
        level = level * jnp.repeat(steps, dims[position] // parts).reshape([-1 if axis == position else 1 for axis in range(len(dims))])
    return level


def gaussian(key, dims, deviation, reach, pieces=(), kind=jnp.bfloat16):
    values = jax.random.normal(key, dims, jnp.float32) * deviation
    if len(pieces) > 0:
        values = levels(key, dims, pieces, -0.22, 0.18) * values
    return jnp.clip(values, min=-reach, max=reach).astype(kind)


def setup_inputs(seed: int = 0) -> dict:
    key_of = jax.random.split(jax.random.key(seed), 4)
    return {
        "sources": gaussian(key_of[0], (NZ, BOXES, NRHS, NB), 1.0, 6.0, ((0, 32), (1, 8)), jnp.float32),
        "leaf_maps": draw_leaf_maps(jax.random.fold_in(key_of[3], 71), 0),
        "mode_ids": draw_mode_ids(jax.random.fold_in(key_of[3], 71), 0),
    }


def hard_dot(left_mat, right_mat):
    return jnp.dot(left_mat.astype(jnp.float32), right_mat.astype(jnp.float32), precision=lax.Precision.HIGHEST, preferred_element_type=jnp.float32)

def cas_table(mode_list, z_index, length_z):
    phase = mode_list[:, None] * z_index[None, :] % length_z
    angle = phase.astype(jnp.float32) * (2.0 * jnp.pi / length_z)
    return (jnp.cos(angle) + jnp.sin(angle)) / jnp.sqrt(jnp.float32(length_z))

def solve_face(a_31, a_33, b_33, b_32, h_3, g_3):
    face = a_33.shape[0]
    system = jnp.eye(face, dtype=jnp.float32) - hard_dot(a_33, b_33)
    wanted = jnp.concatenate([a_31, -hard_dot(a_33, b_32), (h_3 - hard_dot(g_3, a_33.T)).T], axis=1)
    factor = jnp.linalg.cholesky(hard_dot(system.T, system))
    middle = lax.linalg.triangular_solve(factor, hard_dot(system.T, wanted), left_side=True, lower=True)
    solved = lax.linalg.triangular_solve(factor, middle, left_side=True, lower=True, transpose_a=True)
    return (solved[:, :face], solved[:, face:2 * face], solved[:, 2 * face:])

def left_rows(a_11, a_13, b_33, b_32, h_1, g_3, x_one, x_two, x_data):
    top_left = a_11 + hard_dot(a_13, hard_dot(b_33, x_one))
    top_right = hard_dot(a_13, hard_dot(b_33, x_two) - b_32)
    data_left = h_1 + hard_dot(a_13, hard_dot(b_33, x_data) - g_3.T).T
    return (jnp.concatenate([top_left, top_right], axis=1), data_left)

def right_rows(b_23, b_22, g_2, x_one, x_two, x_data):
    low_left = -hard_dot(b_23, x_one)
    low_right = b_22 - hard_dot(b_23, x_two)
    data_right = g_2 - hard_dot(b_23, x_data).T
    return (jnp.concatenate([low_left, low_right], axis=1), data_right)

def merge_full(a_map, b_map, a_data, b_data):
    face = a_map.shape[0] // 2
    x_one, x_two, x_data = solve_face(a_map[face:, :face], a_map[face:, face:], b_map[:face, :face], b_map[:face, face:], a_data[:, face:], b_data[:, :face])
    top_rows, data_left = left_rows(a_map[:face, :face], a_map[:face, face:], b_map[:face, :face], b_map[:face, face:], a_data[:, :face], b_data[:, :face], x_one, x_two, x_data)
    low_rows, data_right = right_rows(b_map[face:, :face], b_map[face:, face:], b_data[:, face:], x_one, x_two, x_data)
    return (jnp.concatenate([top_rows, low_rows], axis=0), jnp.concatenate([data_left, data_right], axis=1))

def reference(sources, leaf_maps, mode_ids):
    cas_rows = cas_table(mode_ids, jnp.arange(NZ, dtype=jnp.int32), NZ)
    spectral = jnp.einsum('mz,zbrp->mbrp', cas_rows, sources, precision=lax.Precision.HIGHEST)

    def per_mode(pair):
        maps_mode, data_mode = pair
        one_map, one_data = jax.vmap(merge_full)(maps_mode[0::2], maps_mode[1::2], data_mode[0::2], data_mode[1::2])
        two_map, two_data = jax.vmap(merge_full)(one_map[0::2], one_map[1::2], one_data[0::2], one_data[1::2])
        count_two = two_map.shape[0]
        map_rows = two_map.reshape(count_two * 2, NP, NB) * jnp.sqrt(jnp.float32(NB))
        data_rows = jnp.transpose(two_data.reshape(count_two, NRHS, 2, NP), (0, 2, 1, 3)).reshape(count_two * 2, NRHS, NP)
        return (map_rows, data_rows)
    merged_map, merged_data = lax.map(per_mode, (leaf_maps, spectral))
    return (merged_map, merged_data)
```

```python
import jax
import jax.numpy as jnp
from jax import lax
from jax.sharding import PartitionSpec as P

NZ = 512


def swapped(block, axis):
    count = lax.axis_size(axis)
    route = []
    for low in range(0, count, 2):
        route += [(low, low + 1), (low + 1, low)]
    return lax.ppermute(block, axis, route)


def mul(left_mat, right_mat):
    return jnp.dot(
        left_mat, right_mat, precision=lax.Precision.HIGH, preferred_element_type=jnp.float32
    )


def mul_rows(rows, mat):
    return lax.dot_general(
        rows,
        mat,
        (((1,), (1,)), ((), ())),
        precision=lax.Precision.HIGH,
        preferred_element_type=jnp.float32,
    )


def cas_table(mode_list, z_index, length_z):
    phase = mode_list[:, None] * z_index[None, :] % length_z
    angle = phase.astype(jnp.float32) * (2.0 * jnp.pi / length_z)
    return (jnp.cos(angle) + jnp.sin(angle)) / jnp.sqrt(jnp.float32(length_z))


def inverse(kernel_map):
    face = kernel_map.shape[0]
    power = mul(kernel_map, kernel_map)
    total = jnp.eye(face, dtype=jnp.float32) + kernel_map

    def again(state):
        return (state[3] > 1e-15) & (state[0] < 64)

    def step(state):
        count, total, power, _ = state
        both = mul(jnp.concatenate([total, power], axis=0), power)
        total = total + both[:face]
        power = both[face:]
        return count + 1, total, power, jnp.sum(power * power)

    state = lax.while_loop(again, step, (0, total, power, jnp.sum(power * power)))
    return state[1]


def local(sources, leaf_maps, mode_ids):
    slab_planes = sources.shape[0]
    points = leaf_maps.shape[-1]
    face = points // 2
    z_index = lax.axis_index("gz") * slab_planes + jnp.arange(slab_planes, dtype=jnp.int32)
    cas_rows = cas_table(mode_ids, z_index, NZ)
    spectral = lax.psum_scatter(
        jnp.einsum("mz,zbrp->mbrp", cas_rows, sources, precision=lax.Precision.HIGH),
        "gz",
        scatter_dimension=0,
        tiled=True,
    )
    far = lax.axis_index("box") % 2
    near = 1 - far

    def block(leaf, row, col):
        return lax.dynamic_slice(
            leaf_maps, (0, leaf, row * face, col * face), (1, 1, face, face)
        ).reshape(face, face)

    def info(leaf, side):
        rows = spectral.shape[2]
        return lax.dynamic_slice(
            spectral, (0, leaf, 0, side * face), (1, 1, rows, face)
        ).reshape(rows, face)

    a_11, a_13 = block(far, far, far), block(far, far, near)
    a_31, a_33 = block(far, near, far), block(far, near, near)
    b_33, b_32 = block(near, far, far), block(near, far, near)
    b_23, b_22 = block(near, near, far), block(near, near, near)
    inv_one = inverse(mul(a_33, b_33))
    through = mul(a_33, b_32)
    near_gain = mul(b_23, inv_one)
    o_33 = b_22 + mul(near_gain, through)
    y_33 = swapped(o_33, "box")
    o_31 = -mul(near_gain, a_31)
    y_32 = swapped(o_31, "box")
    far_gain = mul(mul(a_13, b_33), inv_one)
    o_11 = a_11 + mul(far_gain, a_31)
    o_13 = -mul(a_13, b_32) - mul(far_gain, through)
    h_1, h_3 = info(far, far), info(far, near)
    g_3, g_2 = info(near, far), info(near, near)
    jump = h_3 - mul_rows(g_3, a_33)
    near_data = g_2 - mul_rows(jump, near_gain)
    far_data = h_1 + mul_rows(jump, far_gain) - mul_rows(g_3, a_13)
    other_data = swapped(near_data, "box")
    inv_two = inverse(mul(y_33, o_33))
    gain = mul(o_13, inv_two)
    own = o_11 + mul(gain, mul(y_33, o_31))
    data = far_data + mul_rows(mul_rows(near_data, y_33) - other_data, gain)
    other = -mul(gain, y_32)
    scale = jnp.sqrt(jnp.float32(points))
    is_left = far == 0
    out = jnp.concatenate(
        [jnp.where(is_left, own, other), jnp.where(is_left, other, own)], axis=1
    )
    return ((out * scale)[None, None], data[None, None])


def solution(mesh):
    placed = (P("gz", "box", None, None), P("gz", "box", None, None), P())
    return jax.shard_map(
        local,
        mesh=mesh,
        in_specs=placed,
        out_specs=(P("gz", "box", None, None), P("gz", "box", None, None)),
        check_vma=False,
    )
```

```python
import jax
import jax.numpy as jnp
from jax import lax
from jax.experimental import pallas as pl
from jax.experimental.pallas import tpu as pltpu
from jax.sharding import PartitionSpec as P

NZ = 512
MESH = pl.DeviceIdType.MESH
F32 = jnp.float32
BF16 = jnp.bfloat16
HALF = 256
ROUGH = 4e-4
FINE = 1e-10
VMEM_LIMIT = 44 * 1024 * 1024


def swapped(block, axis):
    count = lax.axis_size(axis)
    route = []
    for low in range(0, count, 2):
        route += [(low, low + 1), (low + 1, low)]
    return lax.ppermute(block, axis, route)


def cas_table(mode_list, z_index, length_z):
    phase = mode_list[:, None] * z_index[None, :] % length_z
    angle = phase.astype(F32) * (2.0 * jnp.pi / length_z)
    return (jnp.cos(angle) + jnp.sin(angle)) / jnp.sqrt(jnp.float32(length_z))


def split(value):
    high = value.astype(BF16)
    return high, (value - high.astype(F32)).astype(BF16)


def put_left(ref, start, value):
    face = value.shape[1]
    high, low = split(value)
    rows = pl.ds(start, value.shape[0])
    ref[rows, 0:face] = high
    ref[rows, face : 2 * face] = high
    ref[rows, 2 * face : 3 * face] = low


def put_right(ref, start, value):
    face = ref.shape[0] // 3
    high, low = split(value)
    count = value.shape[0]
    ref[pl.ds(start, count), :] = high
    ref[pl.ds(face + start, count), :] = low
    ref[pl.ds(2 * face + start, count), :] = high


def fill(put, ref, source):
    for start in range(0, source.shape[0], HALF):
        put(ref, start, source[start : start + HALF, :])


def product(left, right, start):
    return jnp.dot(left[start : start + HALF, :], right[...], preferred_element_type=F32)


def halves(face):
    return range(0, face, HALF)


def eye_rows(start, face):
    row = lax.broadcasted_iota(jnp.int32, (HALF, face), 0) + start
    col = lax.broadcasted_iota(jnp.int32, (HALF, face), 1)
    return jnp.where(row == col, 1.0, 0.0).astype(F32)


def invert(k_left, total, power, rough, left, right, spare):
    face = total.shape[0]

    def square():
        return [
            jnp.dot(power[s : s + HALF, :], power[...], preferred_element_type=F32)
            for s in halves(face)
        ]

    def keep(parts):
        size = 0.0
        for s, part in zip(halves(face), parts):
            power[s : s + HALF, :] = part.astype(BF16)
            size += jnp.sum(part * part)
        return size

    size = keep(square())

    def rough_step(state):
        count, _ = state
        for s in halves(face):
            rough[s : s + HALF, :] = total[s : s + HALF, :].astype(BF16)
        for s in halves(face):
            total[s : s + HALF, :] += jnp.dot(
                rough[s : s + HALF, :], power[...], preferred_element_type=F32
            )
        return count + 1, keep(square())

    lax.while_loop(
        lambda state: (state[1] > ROUGH) & (state[0] < 12), rough_step, (jnp.int32(0), size)
    )

    def residual():
        size = 0.0
        fill(put_right, right, total)
        for s in halves(face):
            part = (
                product(k_left, right, s) - total[s : s + HALF, :] + eye_rows(s, face)
            )
            spare[s : s + HALF, :] = part
            size += jnp.sum(part * part)
        return size

    first = residual()
    bad = jnp.logical_not(first < 0.25)

    def careful():
        for s in halves(face):
            kept = k_left[s : s + HALF, 0:face].astype(F32)
            kept += k_left[s : s + HALF, 2 * face : 3 * face].astype(F32)
            spare[s : s + HALF, :] = kept
            total[s : s + HALF, :] = kept + eye_rows(s, face)

        def raise_power():
            fill(put_left, left, spare)
            fill(put_right, right, spare)
            size = 0.0
            for s in halves(face):
                part = product(left, right, s)
                spare[s : s + HALF, :] = part
                size += jnp.sum(part * part)
            return size

        def step(state):
            count, _ = state
            fill(put_left, left, total)
            fill(put_right, right, spare)
            for s in halves(face):
                total[s : s + HALF, :] += product(left, right, s)
            return count + 1, raise_power()

        lax.while_loop(
            lambda state: (state[1] > 1e-15) & (state[0] < 48),
            step,
            (jnp.int32(0), raise_power()),
        )
        return residual()

    first = lax.cond(bad, careful, lambda: first)

    def newton(state):
        count, size, _ = state
        for s in halves(face):
            rough[s : s + HALF, :] = spare[s : s + HALF, :].astype(BF16)
        second = 0.0
        for s in halves(face):
            part = jnp.dot(rough[s : s + HALF, :], rough[...], preferred_element_type=F32)
            second += jnp.sum(part * part)
            put_right(right, s, spare[s : s + HALF, :] + part)
        fill(put_left, left, total)
        for s in halves(face):
            total[s : s + HALF, :] += product(left, right, s)
        bound = size * second
        size = lax.cond(bound > FINE, residual, lambda: size)
        return count + 1, size, bound

    lax.while_loop(
        lambda state: (state[2] > FINE) & (state[0] < 12),
        newton,
        (jnp.int32(0), first, jnp.float32(1.0)),
    )


def near_kernel(maps, o_33, o_31, gain, inv, through, *scratch):
    a_33, b_33, b_32, b_23, b_22, a_31 = scratch[:6]
    l_one, l_two, k_left, r_one, r_two, power, rough, spare, sems = scratch[6:]
    face = o_33.shape[0]
    far = lax.axis_index("box") % 2
    near = 1 - far

    def fetch(slot, leaf, row, col, dst):
        view = maps.at[
            0,
            leaf,
            pl.ds(pl.multiple_of(row * face, face), face),
            pl.ds(pl.multiple_of(col * face, face), face),
        ]
        copy = pltpu.make_async_copy(view, dst, sems.at[slot])
        copy.start()
        return copy

    copies = [
        fetch(0, far, near, near, a_33),
        fetch(1, near, far, far, b_33),
        fetch(2, near, far, near, b_32),
        fetch(3, near, near, far, b_23),
        fetch(4, near, near, near, b_22),
        fetch(5, far, near, far, a_31),
    ]
    copies[0].wait()
    fill(put_left, l_one, a_33)
    copies[1].wait()
    fill(put_right, r_one, b_33)
    for s in halves(face):
        part = product(l_one, r_one, s)
        put_left(k_left, s, part)
        power[s : s + HALF, :] = part.astype(BF16)
        inv[s : s + HALF, :] = part + eye_rows(s, face)
    copies[2].wait()
    fill(put_right, r_one, b_32)
    for s in halves(face):
        part = product(l_one, r_one, s)
        through[s : s + HALF, :] = part
    fill(put_right, r_two, through)
    invert(k_left, inv, power, rough, l_one, r_one, spare)
    copies[3].wait()
    fill(put_left, l_one, b_23)
    fill(put_right, r_one, inv)
    for s in halves(face):
        part = product(l_one, r_one, s)
        gain[s : s + HALF, :] = part
        put_left(l_two, s, part)
    copies[4].wait()
    for s in halves(face):
        o_33[s : s + HALF, :] = b_22[s : s + HALF, :] + product(l_two, r_two, s)
    copies[5].wait()
    fill(put_right, r_one, a_31)
    for s in halves(face):
        o_31[s : s + HALF, :] = -product(l_two, r_one, s)


def far_kernel(maps, inv, through, o_11, o_13, gain, *scratch):
    a_13, b_33, b_32, a_11, a_31, left, r_one, r_two, sems = scratch
    face = o_11.shape[0]
    far = lax.axis_index("box") % 2
    near = 1 - far

    def fetch(slot, leaf, row, col, dst):
        view = maps.at[
            0,
            leaf,
            pl.ds(pl.multiple_of(row * face, face), face),
            pl.ds(pl.multiple_of(col * face, face), face),
        ]
        copy = pltpu.make_async_copy(view, dst, sems.at[slot])
        copy.start()
        return copy

    copies = [
        fetch(0, far, far, near, a_13),
        fetch(1, near, far, far, b_33),
        fetch(2, near, far, near, b_32),
        fetch(3, far, far, far, a_11),
        fetch(4, far, near, far, a_31),
    ]
    copies[0].wait()
    fill(put_left, left, a_13)
    copies[1].wait()
    fill(put_right, r_one, b_33)
    copies[2].wait()
    fill(put_right, r_two, b_32)
    for s in halves(face):
        gain[s : s + HALF, :] = product(left, r_one, s)
        o_13[s : s + HALF, :] = -product(left, r_two, s)
    fill(put_left, left, gain)
    fill(put_right, r_one, inv)
    for s in halves(face):
        gain[s : s + HALF, :] = product(left, r_one, s)
    fill(put_left, left, gain)
    copies[4].wait()
    fill(put_right, r_one, a_31)
    fill(put_right, r_two, through)
    copies[3].wait()
    for s in halves(face):
        o_11[s : s + HALF, :] = a_11[s : s + HALF, :] + product(left, r_one, s)
        o_13[s : s + HALF, :] -= product(left, r_two, s)


def rows_times(rows, mat):
    r_high, r_low = split(rows)
    m_high, m_low = split(mat)

    def dot(left, right):
        return lax.dot_general(
            left, right, (((1,), (1,)), ((), ())), preferred_element_type=F32
        )

    return dot(r_high, m_high) + (dot(r_low, m_high) + dot(r_high, m_low))


def data_kernel(maps, spectral, near_gain, far_gain, near_data, far_data, a_33, a_13, sems):
    face = near_gain.shape[0]
    far = lax.axis_index("box") % 2
    near = 1 - far

    def fetch(slot, leaf, row, col, dst):
        view = maps.at[
            0,
            leaf,
            pl.ds(pl.multiple_of(row * face, face), face),
            pl.ds(pl.multiple_of(col * face, face), face),
        ]
        copy = pltpu.make_async_copy(view, dst, sems.at[slot])
        copy.start()
        return copy

    copies = [fetch(0, far, near, near, a_33), fetch(1, far, far, near, a_13)]

    def info(leaf, side):
        return spectral[leaf, :, pl.ds(pl.multiple_of(side * face, face), face)]

    h_1, h_3 = info(far, far), info(far, near)
    g_3, g_2 = info(near, far), info(near, near)
    copies[0].wait()
    jump = h_3 - rows_times(g_3, a_33[...])
    near_data[...] = g_2 - rows_times(jump, near_gain[...])
    copies[1].wait()
    far_data[...] = h_1 + rows_times(jump, far_gain[...]) - rows_times(g_3, a_13[...])


def top_kernel(y_33, o_33, o_31, o_13, o_11, out, gain, *scratch):
    own, inv, l_one, k_left, r_one, r_two, power, rough, spare, sem = scratch
    face = y_33.shape[0]
    far = lax.axis_index("box") % 2
    fill(put_left, l_one, y_33)
    fill(put_right, r_one, o_33)
    for s in halves(face):
        part = product(l_one, r_one, s)
        put_left(k_left, s, part)
        power[s : s + HALF, :] = part.astype(BF16)
        inv[s : s + HALF, :] = part + eye_rows(s, face)
    fill(put_right, r_one, o_31)
    for s in halves(face):
        put_right(r_two, s, product(l_one, r_one, s))
    invert(k_left, inv, power, rough, l_one, r_one, spare)
    fill(put_left, l_one, o_13)
    fill(put_right, r_one, inv)
    for s in halves(face):
        part = product(l_one, r_one, s)
        gain[s : s + HALF, :] = part
        put_left(k_left, s, part)
    scale = (2.0 * face) ** 0.5
    for s in halves(face):
        own[s : s + HALF, :] = (o_11[s : s + HALF, :] + product(k_left, r_two, s)) * scale
    copy = pltpu.make_async_copy(
        own, out.at[:, pl.ds(pl.multiple_of(far * face, face), face)], sem
    )
    copy.start()
    copy.wait()


def last_kernel(
    y_32, gain, y_33, near_data, far_data, other_data, _, out, data, other, left, right, sem
):
    face = gain.shape[0]
    near = 1 - lax.axis_index("box") % 2
    scale = (2.0 * face) ** 0.5
    fill(put_left, left, gain)
    fill(put_right, right, y_32)
    for s in halves(face):
        other[s : s + HALF, :] = product(left, right, s) * -scale
    copy = pltpu.make_async_copy(
        other, out.at[:, pl.ds(pl.multiple_of(near * face, face), face)], sem
    )
    copy.start()
    jump = rows_times(near_data[...], y_33[...]) - other_data[...]
    data[...] = far_data[...] + rows_times(jump, gain[...])
    copy.wait()


def sums_kernel(cas, own, other, out, sent, got, mine, side_sent, side_got, send_sem, recv_sem):
    planes = own.shape[0]
    here = lax.axis_index("gz")
    core, z, x = here % 2, here // 2 % 8, here // 16

    def device(x_at, z_at):
        return {"gz": x_at * 16 + z_at * 2 + core}

    ring = (device(x, (z + 1) % 8), device(x, (z + 7) % 8))
    beside = device(1 - x, z)
    barrier = pltpu.get_barrier_semaphore()
    for target in (*ring, beside):
        pl.semaphore_signal(barrier, inc=1, device_id=target, device_id_type=MESH)

    def term(x_to, z_to, store):
        row = (x_to * 8 + z_to) * (2 * planes)

        def block(part, carry):
            rows = pl.ds(pl.multiple_of(part * 8, 8), 8)
            total = cas[row] * own[0, rows, :]
            for k in range(1, planes):
                total += cas[row + k] * own[k, rows, :]
            for k in range(planes):
                total += cas[row + planes + k] * other[k, rows, :]
            store(rows, total)
            return carry

        lax.fori_loop(0, own.shape[1] // 8, block, 0)

    def message(way, index):
        return pltpu.make_async_remote_copy(
            src_ref=sent.at[way, index],
            dst_ref=got.at[way, index],
            send_sem=send_sem.at[way, index],
            recv_sem=recv_sem.at[way, index],
            device_id=ring[way],
            device_id_type=MESH,
        )

    copies = [[message(way, index) for index in range(7)] for way in range(2)]
    for index in range(7):
        step = (index + 3) // 2
        first = index % 2 == 0
        for way in range(2):
            x_to = way if first else 1 - way
            z_to = (z + (5 - step)) % 8 if way == 0 else (z + 8 - (5 - step)) % 8

            def store(rows, total, way=way, index=index):
                sent[way, index, rows, :] = total

            term(x_to, z_to, store)
            if index == 0 and way == 0:
                pl.semaphore_wait(barrier, 3)
            if index >= 2:
                copies[way][index - 2].wait_recv()
                sent[way, index] += got[way, index - 2]
            copies[way][index].start()
    for x_to in range(2):

        def store(rows, total, x_to=x_to):
            mine[x_to, rows, :] = total

        term(x_to, z, store)
    for index in (5, 6):
        for way in range(2):
            copies[way][index].wait_recv()
    away = 1 - x
    side_sent[...] = mine[away] + (got[0, 6 - away] + got[1, 5 + away])
    last = pltpu.make_async_remote_copy(
        src_ref=side_sent,
        dst_ref=side_got,
        send_sem=send_sem.at[2, 0],
        recv_sem=recv_sem.at[2, 0],
        device_id=beside,
        device_id_type=MESH,
    )
    last.start()
    mine[x] += got[0, 6 - x] + got[1, 5 + x]
    last.wait_recv()
    out[...] = mine[x] + side_got[...]
    for way in range(2):
        for index in range(7):
            copies[way][index].wait_send()
    last.wait_send()


def vmem_specs(count):
    return [pl.BlockSpec(memory_space=pltpu.VMEM)] * count


ANY = pl.BlockSpec(memory_space=pl.ANY)


def local(sources, leaf_maps, mode_ids):
    planes, boxes, rhs, points = sources.shape
    face = points // 2
    square = jax.ShapeDtypeStruct((face, face), F32)
    rows = jax.ShapeDtypeStruct((rhs, face), F32)
    full = pltpu.VMEM((face, face), F32)
    short = pltpu.VMEM((face, face), BF16)
    left = pltpu.VMEM((face, 3 * face), BF16)
    right = pltpu.VMEM((3 * face, face), BF16)
    params = pltpu.CompilerParams(vmem_limit_bytes=VMEM_LIMIT)

    def cost(units, size):
        return pl.CostEstimate(
            flops=units * 2 * face**3, bytes_accessed=size * 4 * face**2, transcendentals=0
        )

    here = lax.axis_index("gz")
    other_sources = swapped(sources, "gz")
    o_33, o_31, near_gain, inv, through = pl.pallas_call(
        near_kernel,
        out_shape=[square] * 5,
        in_specs=[ANY],
        out_specs=vmem_specs(5),
        scratch_shapes=[full] * 6
        + [left, left, left, right, right, short, short, full, pltpu.SemaphoreType.DMA((6,))],
        compiler_params=params,
        cost_estimate=cost(30, 11),
        name="level_one_near",
    )(leaf_maps)
    y_33 = swapped(o_33, "box")
    y_32 = swapped(o_31, "box")
    core = here % 2
    modes = lax.dynamic_slice(mode_ids.reshape(-1, 2), (0, core), (16, 1)).reshape(16)
    lanes = jnp.arange(planes, dtype=jnp.int32)
    z_index = jnp.concatenate([here * planes + lanes, (here + 1 - 2 * core) * planes + lanes])
    cas = cas_table(modes, z_index, NZ).reshape(-1)
    lines = boxes * rhs
    line = (lines, points)
    spectral = pl.pallas_call(
        sums_kernel,
        out_shape=jax.ShapeDtypeStruct(line, F32),
        in_specs=[pl.BlockSpec(memory_space=pltpu.SMEM)] + vmem_specs(2),
        out_specs=vmem_specs(1)[0],
        scratch_shapes=[
            pltpu.VMEM((2, 7, *line), F32),
            pltpu.VMEM((2, 7, *line), F32),
            pltpu.VMEM((2, *line), F32),
            pltpu.VMEM(line, F32),
            pltpu.VMEM(line, F32),
            pltpu.SemaphoreType.DMA((3, 7)),
            pltpu.SemaphoreType.DMA((3, 7)),
        ],
        compiler_params=pltpu.CompilerParams(
            vmem_limit_bytes=VMEM_LIMIT, collective_id=0, has_side_effects=True
        ),
        cost_estimate=cost(100, 5),
        name="hartley_sums",
    )(cas, sources.reshape(planes, *line), other_sources.reshape(planes, *line))
    o_11, o_13, far_gain = pl.pallas_call(
        far_kernel,
        out_shape=[square] * 3,
        in_specs=[ANY] + vmem_specs(2),
        out_specs=vmem_specs(3),
        scratch_shapes=[full] * 5 + [left, right, right, pltpu.SemaphoreType.DMA((5,))],
        compiler_params=params,
        cost_estimate=cost(15, 10),
        name="level_one_far",
    )(leaf_maps, inv, through)
    near_data, far_data = pl.pallas_call(
        data_kernel,
        out_shape=[rows] * 2,
        in_specs=[ANY] + vmem_specs(3),
        out_specs=vmem_specs(2),
        scratch_shapes=[full] * 2 + [pltpu.SemaphoreType.DMA((2,))],
        compiler_params=params,
        cost_estimate=cost(2, 4),
        name="level_one_data",
    )(leaf_maps, spectral.reshape(boxes, rhs, points), near_gain, far_gain)
    other_data = swapped(near_data, "box")
    out, gain = pl.pallas_call(
        top_kernel,
        out_shape=[jax.ShapeDtypeStruct((face, points), F32), square],
        in_specs=vmem_specs(5),
        out_specs=[ANY] + vmem_specs(1),
        scratch_shapes=[full, full, left, left, right, right, short, short, full]
        + [pltpu.SemaphoreType.DMA],
        compiler_params=params,
        cost_estimate=cost(25, 8),
        name="level_two_gain",
    )(y_33, o_33, o_31, o_13, o_11)
    out, data = pl.pallas_call(
        last_kernel,
        out_shape=[jax.ShapeDtypeStruct((face, points), F32), rows],
        in_specs=vmem_specs(6) + [ANY],
        out_specs=[ANY] + vmem_specs(1),
        scratch_shapes=[full, left, right, pltpu.SemaphoreType.DMA],
        input_output_aliases={6: 0},
        compiler_params=params,
        cost_estimate=cost(4, 5),
        name="level_two_rows",
    )(y_32, gain, y_33, near_data, far_data, other_data, out)
    return (out[None, None], data[None, None])


def solution(mesh):
    placed = (P("gz", "box", None, None), P("gz", "box", None, None), P())
    return jax.shard_map(
        local,
        mesh=mesh,
        in_specs=placed,
        out_specs=(P("gz", "box", None, None), P("gz", "box", None, None)),
        check_vma=False,
    )
```

```python
import jax
import jax.numpy as jnp
from jax import lax
from jax.experimental import pallas as pl
from jax.experimental.pallas import tpu as pltpu
from jax.sharding import PartitionSpec as P

NZ = 512
MESH = pl.DeviceIdType.MESH
F32 = jnp.float32
BF16 = jnp.bfloat16
HALF = 256
FINE = 3.6e-9
VMEM_LIMIT = 60 * 1024 * 1024
LESS_VMEM = 50 * 1024 * 1024
LAST_VMEM = 28 * 1024 * 1024


def swapped(block, axis):
    count = lax.axis_size(axis)
    route = []
    for low in range(0, count, 2):
        route += [(low, low + 1), (low + 1, low)]
    return lax.ppermute(block, axis, route)


def cas_table(mode_list, z_index, length_z):
    phase = mode_list[:, None] * z_index[None, :] % length_z
    angle = phase.astype(F32) * (2.0 * jnp.pi / length_z)
    return (jnp.cos(angle) + jnp.sin(angle)) / jnp.sqrt(jnp.float32(length_z))


def split(value):
    high = value.astype(BF16)
    return high, (value - high.astype(F32)).astype(BF16)


def put_left(ref, start, value):
    face = value.shape[1]
    high, low = split(value)
    rows = pl.ds(start, value.shape[0])
    ref[rows, 0:face] = high
    ref[rows, face : 2 * face] = high
    ref[rows, 2 * face : 3 * face] = low


def put_right(ref, start, value):
    face = ref.shape[0] // 3
    high, low = split(value)
    count = value.shape[0]
    ref[pl.ds(start, count), :] = high
    ref[pl.ds(face + start, count), :] = low
    ref[pl.ds(2 * face + start, count), :] = high


def fill(put, ref, source):
    for start in range(0, source.shape[0], HALF):
        put(ref, start, source[start : start + HALF, :])


def product(left, right, start):
    return jnp.dot(left[start : start + HALF, :], right[...], preferred_element_type=F32)


def halves(face):
    return range(0, face, HALF)


def eye_rows(start, face):
    row = lax.broadcasted_iota(jnp.int32, (HALF, face), 0) + start
    col = lax.broadcasted_iota(jnp.int32, (HALF, face), 1)
    return jnp.where(row == col, 1.0, 0.0).astype(F32)


def chunk_sum(part):
    return jnp.sum(part.reshape(-1, 8, part.shape[1]), axis=0)


def invert(k_left, total, power, rough, left, right, spare):
    face = total.shape[0]

    def raise_power():
        parts = [
            jnp.dot(power[s : s + HALF, :], power[...], preferred_element_type=F32)
            for s in halves(face)
        ]
        for s, part in zip(halves(face), parts):
            power[s : s + HALF, :] = part.astype(BF16)

    def gather():
        for s in halves(face):
            rough[s : s + HALF, :] = total[s : s + HALF, :].astype(BF16)
        for s in halves(face):
            total[s : s + HALF, :] += jnp.dot(
                rough[s : s + HALF, :], power[...], preferred_element_type=F32
            )

    raise_power()
    for _ in range(3):
        gather()
        raise_power()
    gather()
    for s in halves(face):
        rough[s : s + HALF, :] = total[s : s + HALF, :].astype(BF16)
    first = jnp.zeros((8, face), F32)
    for s in halves(face):
        part = jnp.dot(
            k_left[s : s + HALF, 0:face], rough[...], preferred_element_type=F32
        ) + jnp.dot(
            k_left[s : s + HALF, 2 * face : 3 * face], rough[...], preferred_element_type=F32
        )
        part = part - rough[s : s + HALF, :].astype(F32) + eye_rows(s, face)
        spare[s : s + HALF, :] = part
        power[s : s + HALF, :] = part.astype(BF16)
        first += chunk_sum(part * part)
    second = jnp.zeros((8, face), F32)
    for s in halves(face):
        part = jnp.dot(power[s : s + HALF, :], power[...], preferred_element_type=F32)
        second += chunk_sum(part * part)
        spare[s : s + HALF, :] += part
    for s in halves(face):
        power[s : s + HALF, :] = spare[s : s + HALF, :].astype(BF16)
    for s in halves(face):
        total[s : s + HALF, :] = rough[s : s + HALF, :].astype(F32) + jnp.dot(
            rough[s : s + HALF, :], power[...], preferred_element_type=F32
        )
    first, second = jnp.sum(first), jnp.sum(second)

    @pl.when(jnp.logical_not((first < 0.25) & (first * second < FINE)))
    def _():
        careful(k_left, total, left, right, spare)


def careful(k_left, total, left, right, spare):
    face = total.shape[0]
    for s in halves(face):
        kept = k_left[s : s + HALF, 0:face].astype(F32)
        kept += k_left[s : s + HALF, 2 * face : 3 * face].astype(F32)
        spare[s : s + HALF, :] = kept
        total[s : s + HALF, :] = kept + eye_rows(s, face)

    def raise_power():
        fill(put_left, left, spare)
        fill(put_right, right, spare)
        size = 0.0
        for s in halves(face):
            part = product(left, right, s)
            spare[s : s + HALF, :] = part
            size += jnp.sum(part * part)
        return size

    def squaring(state):
        count, _ = state
        fill(put_left, left, total)
        fill(put_right, right, spare)
        for s in halves(face):
            total[s : s + HALF, :] += product(left, right, s)
        return count + 1, raise_power()

    lax.while_loop(
        lambda state: (state[1] > 1e-15) & (state[0] < 48),
        squaring,
        (jnp.int32(0), raise_power()),
    )

    def newton(state):
        count, last, _ = state
        fill(put_right, right, total)
        size = 0.0
        for s in halves(face):
            part = product(k_left, right, s) - total[s : s + HALF, :] + eye_rows(s, face)
            spare[s : s + HALF, :] = part
            size += jnp.sum(part * part)
        better = size < 0.25 * last

        @pl.when(better)
        def _():
            fill(put_left, left, total)
            fill(put_right, right, spare)
            for s in halves(face):
                total[s : s + HALF, :] += product(left, right, s)

        return count + 1, size, better

    lax.while_loop(
        lambda state: state[2] & (state[0] < 4),
        newton,
        (jnp.int32(0), jnp.float32(1.0), jnp.bool_(True)),
    )


def fetcher(maps, sems, face):
    def fetch(slot, leaf, row, col, dst):
        copy = pltpu.make_async_copy(
            maps.at[
                0,
                leaf,
                pl.ds(pl.multiple_of(row * face, face), face),
                pl.ds(pl.multiple_of(col * face, face), face),
            ],
            dst,
            sems.at[slot],
        )
        copy.start()
        return copy

    return fetch


def started(src, dst, sem):
    copy = pltpu.make_async_copy(src, dst, sem)
    copy.start()
    return copy


def near_kernel(maps, o_33_out, o_31_out, gain_out, inv_out, through_out, *scratch):
    a_33, b_33, b_32, b_23, b_22, a_31, gain, inv, through = scratch[:9]
    l_one, l_two, k_left, r_one, r_two, power, rough, spare, sems = scratch[9:]
    face = a_33.shape[0]
    far = lax.axis_index("box") % 2
    near = 1 - far
    fetch = fetcher(maps, sems, face)
    copies = [
        fetch(0, far, near, near, a_33),
        fetch(1, near, far, far, b_33),
        fetch(2, near, far, near, b_32),
        fetch(3, near, near, far, b_23),
        fetch(4, near, near, near, b_22),
        fetch(5, far, near, far, a_31),
    ]
    copies[0].wait()
    fill(put_left, l_one, a_33)
    copies[1].wait()
    fill(put_right, r_one, b_33)
    for s in halves(face):
        part = product(l_one, r_one, s)
        put_left(k_left, s, part)
        power[s : s + HALF, :] = part.astype(BF16)
        inv[s : s + HALF, :] = part + eye_rows(s, face)
    copies[2].wait()
    fill(put_right, r_one, b_32)
    for s in halves(face):
        part = product(l_one, r_one, s)
        through[s : s + HALF, :] = part
        put_right(r_two, s, part)
    outs = [started(through, through_out, sems.at[6])]
    invert(k_left, inv, power, rough, l_one, r_one, spare)
    outs.append(started(inv, inv_out, sems.at[7]))
    copies[3].wait()
    fill(put_left, l_one, b_23)
    fill(put_right, r_one, inv)
    for s in halves(face):
        part = product(l_one, r_one, s)
        gain[s : s + HALF, :] = part
        put_left(l_two, s, part)
    outs.append(started(gain, gain_out, sems.at[8]))
    copies[4].wait()
    for s in halves(face):
        b_22[s : s + HALF, :] += product(l_two, r_two, s)
    outs.append(started(b_22, o_33_out, sems.at[9]))
    copies[5].wait()
    fill(put_right, r_one, a_31)
    for s in halves(face):
        a_31[s : s + HALF, :] = -product(l_two, r_one, s)
    outs.append(started(a_31, o_31_out, sems.at[10]))
    for copy in outs:
        copy.wait()


def keep_pair(highs, lows, start, value):
    high, low = split(value)
    highs[start : start + value.shape[0], :] = high
    lows[start : start + value.shape[0], :] = low


def rows_times(rows, highs, lows):
    r_high, r_low = split(rows)

    def dot(left, right):
        return lax.dot_general(
            left, right, (((1,), (1,)), ((), ())), preferred_element_type=F32
        )

    return dot(r_high, highs[...]) + (dot(r_low, highs[...]) + dot(r_high, lows[...]))


def top_kernel(y_33_in, o_33_in, o_31_in, o_13_in, o_11_in, out, gain_out, *scratch):
    y_33, o_33, o_31, o_13, o_11, gain, inv = scratch[:7]
    l_one, k_left, r_one, r_two, power, rough, spare, sems = scratch[7:]
    face = y_33.shape[0]
    far = lax.axis_index("box") % 2
    copies = [
        started(src, dst, sems.at[slot])
        for slot, (src, dst) in enumerate(
            (
                (y_33_in, y_33),
                (o_33_in, o_33),
                (o_31_in, o_31),
                (o_13_in, o_13),
                (o_11_in, o_11),
            )
        )
    ]
    copies[0].wait()
    fill(put_left, l_one, y_33)
    copies[1].wait()
    fill(put_right, r_one, o_33)
    for s in halves(face):
        part = product(l_one, r_one, s)
        put_left(k_left, s, part)
        power[s : s + HALF, :] = part.astype(BF16)
        inv[s : s + HALF, :] = part + eye_rows(s, face)
    copies[2].wait()
    fill(put_right, r_one, o_31)
    for s in halves(face):
        put_right(r_two, s, product(l_one, r_one, s))
    invert(k_left, inv, power, rough, l_one, r_one, spare)
    copies[3].wait()
    fill(put_left, l_one, o_13)
    fill(put_right, r_one, inv)
    for s in halves(face):
        part = product(l_one, r_one, s)
        gain[s : s + HALF, :] = part
        put_left(k_left, s, part)
    last = [started(gain, gain_out, sems.at[5])]
    scale = (2.0 * face) ** 0.5
    copies[4].wait()
    for s in halves(face):
        o_11[s : s + HALF, :] = (o_11[s : s + HALF, :] + product(k_left, r_two, s)) * scale
        last.append(
            started(
                o_11.at[s : s + HALF, :],
                out.at[s : s + HALF, pl.ds(pl.multiple_of(far * face, face), face)],
                sems.at[6 + s // HALF],
            )
        )
    for copy in last:
        copy.wait()


def last_kernel(
    y_32, gain, y_33, near_data, far_data, other_data, _, out, data, other, left, right, sems
):
    face = gain.shape[0]
    near = 1 - lax.axis_index("box") % 2
    scale = (2.0 * face) ** 0.5
    fill(put_left, left, gain)
    fill(put_right, right, y_32)
    copies = []
    for s in halves(face):
        other[s : s + HALF, :] = product(left, right, s) * -scale
        copies.append(
            started(
                other.at[s : s + HALF, :],
                out.at[s : s + HALF, pl.ds(pl.multiple_of(near * face, face), face)],
                sems.at[s // HALF],
            )
        )
    jump = rows_times(near_data[...], *split(y_33[...])) - other_data[...]
    data[...] = far_data[...] + rows_times(jump, *split(gain[...]))
    for copy in copies:
        copy.wait()


def sums_kernel(
    cas, own_in, other_in, maps, inv_in, through_in, near_gain_in, o_11_out, o_13_out, *scratch
):
    near_data, far_data, sent, got, mine, side_sent, side_got, send_sem, recv_sem = scratch[:9]
    a_13, b_33, b_32, a_11, a_31, a_33, inv, through, near_gain, gain, o_13 = scratch[9:20]
    left, r_one, r_two, near_high, near_low, far_high, far_low, own, other, sems = scratch[20:]
    face = inv.shape[0]
    far = lax.axis_index("box") % 2
    near = 1 - far
    fetch = fetcher(maps, sems, face)
    planes_in = (started(own_in, own, sems.at[11]), started(other_in, other, sems.at[12]))
    copies_in = [
        fetch(0, far, far, near, a_13),
        fetch(1, near, far, far, b_33),
        fetch(2, near, far, near, b_32),
        started(inv_in, inv, sems.at[3]),
        fetch(4, far, near, far, a_31),
        fetch(5, far, far, far, a_11),
        started(through_in, through, sems.at[6]),
        fetch(7, far, near, near, a_33),
        started(near_gain_in, near_gain, sems.at[8]),
    ]
    planes = own.shape[0]
    here = lax.axis_index("gz")
    core, z, x = here % 2, here // 2 % 8, here // 16

    def device(x_at, z_at):
        return {"gz": x_at * 16 + z_at * 2 + core}

    ring = (device(x, (z + 1) % 8), device(x, (z + 7) % 8))
    beside = device(1 - x, z)
    barrier = pltpu.get_barrier_semaphore()
    for target in (*ring, beside):
        pl.semaphore_signal(barrier, inc=1, device_id=target, device_id_type=MESH)
    for copy in planes_in:
        copy.wait()

    def term(x_to, z_to, store):
        row = (x_to * 8 + z_to) * (2 * planes)

        def block(part, carry):
            rows = pl.ds(pl.multiple_of(part * 8, 8), 8)
            total = cas[row] * own[0, rows, :]
            for k in range(1, planes):
                total += cas[row + k] * own[k, rows, :]
            for k in range(planes):
                total += cas[row + planes + k] * other[k, rows, :]
            store(rows, total)
            return carry

        lax.fori_loop(0, own.shape[1] // 8, block, 0)

    def message(way, index):
        return pltpu.make_async_remote_copy(
            src_ref=sent.at[way, index],
            dst_ref=got.at[way, index],
            send_sem=send_sem.at[way, index],
            recv_sem=recv_sem.at[way, index],
            device_id=ring[way],
            device_id_type=MESH,
        )

    copies_out = []

    def work_0():
        copies_in[0].wait()
        fill(put_left, left, a_13)
        copies_in[1].wait()
        fill(put_right, r_one, b_33)
        for s in halves(face):
            gain[s : s + HALF, :] = product(left, r_one, s)

    def work_1():
        copies_in[2].wait()
        fill(put_right, r_two, b_32)
        for s in halves(face):
            o_13[s : s + HALF, :] = -product(left, r_two, s)

    def work_2():
        copies_in[3].wait()
        fill(put_left, left, gain)
        fill(put_right, r_one, inv)
        for s in halves(face):
            gain[s : s + HALF, :] = product(left, r_one, s)

    def work_3():
        fill(put_left, left, gain)
        copies_in[4].wait()
        copies_in[5].wait()
        fill(put_right, r_one, a_31)
        for s in halves(face):
            a_11[s : s + HALF, :] += product(left, r_one, s)
        copies_out.append(started(a_11, o_11_out, sems.at[9]))

    def work_4():
        copies_in[6].wait()
        fill(put_right, r_two, through)
        for s in halves(face):
            o_13[s : s + HALF, :] -= product(left, r_two, s)
        copies_out.append(started(o_13, o_13_out, sems.at[10]))

    def work_5():
        copies_in[7].wait()
        copies_in[8].wait()
        for s in halves(face):
            rows = slice(s, s + HALF)
            keep_pair(far_high, far_low, s, a_33[rows, :])
            keep_pair(far_high, far_low, face + s, a_13[rows, :])
            keep_pair(near_high, near_low, s, near_gain[rows, :])
            keep_pair(near_high, near_low, face + s, gain[rows, :])

    work = (work_0, work_1, work_2, work_3, work_4, work_5, lambda: None)
    copies = [[message(way, index) for index in range(7)] for way in range(2)]
    for index in range(7):
        step = (index + 3) // 2
        first = index % 2 == 0
        for way in range(2):
            x_to = way if first else 1 - way
            z_to = (z + (5 - step)) % 8 if way == 0 else (z + 8 - (5 - step)) % 8

            def store(rows, total, way=way, index=index):
                sent[way, index, rows, :] = total

            term(x_to, z_to, store)
            if index == 0 and way == 0:
                pl.semaphore_wait(barrier, 3)
            if index >= 2:
                copies[way][index - 2].wait_recv()
                sent[way, index] += got[way, index - 2]
            copies[way][index].start()
        work[index]()
    for x_to in range(2):

        def store(rows, total, x_to=x_to):
            mine[x_to, rows, :] = total

        term(x_to, z, store)
    for index in (5, 6):
        for way in range(2):
            copies[way][index].wait_recv()
    away = 1 - x
    side_sent[...] = mine[away] + (got[0, 6 - away] + got[1, 5 + away])
    last = pltpu.make_async_remote_copy(
        src_ref=side_sent,
        dst_ref=side_got,
        send_sem=send_sem.at[2, 0],
        recv_sem=recv_sem.at[2, 0],
        device_id=beside,
        device_id_type=MESH,
    )
    last.start()
    mine[x] += got[0, 6 - x] + got[1, 5 + x]
    last.wait_recv()
    mine[x] += side_got[...]
    rhs = near_data.shape[0]

    def info(leaf, side):
        return mine[
            x,
            pl.ds(pl.multiple_of(leaf * rhs, rhs), rhs),
            pl.ds(pl.multiple_of(side * face, face), face),
        ]

    known = rows_times(info(near, far), far_high, far_low)
    jump = info(far, near) - known[:, 0:face]
    moved = rows_times(jump, near_high, near_low)
    near_data[...] = info(near, near) - moved[:, 0:face]
    far_data[...] = info(far, far) + moved[:, face : 2 * face] - known[:, face : 2 * face]
    for way in range(2):
        for index in range(7):
            copies[way][index].wait_send()
    last.wait_send()
    for copy in copies_out:
        copy.wait()


def vmem_specs(count):
    return [pl.BlockSpec(memory_space=pltpu.VMEM)] * count


ANY = pl.BlockSpec(memory_space=pl.ANY)


def local(sources, leaf_maps, mode_ids):
    planes, boxes, rhs, points = sources.shape
    face = points // 2
    square = jax.ShapeDtypeStruct((face, face), F32)
    rows = jax.ShapeDtypeStruct((rhs, face), F32)
    full = pltpu.VMEM((face, face), F32)
    short = pltpu.VMEM((face, face), BF16)
    left = pltpu.VMEM((face, 3 * face), BF16)
    right = pltpu.VMEM((3 * face, face), BF16)
    params = pltpu.CompilerParams(vmem_limit_bytes=VMEM_LIMIT)

    def cost(units, size):
        return pl.CostEstimate(
            flops=units * 2 * face**3, bytes_accessed=size * 4 * face**2, transcendentals=0
        )

    here = lax.axis_index("gz")
    other_sources = swapped(sources, "gz")
    o_33, o_31, near_gain, inv, through = pl.pallas_call(
        near_kernel,
        out_shape=[square] * 5,
        in_specs=[ANY],
        out_specs=[ANY] * 5,
        scratch_shapes=[full] * 9
        + [left, left, left, right, right, short, short, full, pltpu.SemaphoreType.DMA((11,))],
        compiler_params=params,
        cost_estimate=cost(27, 11),
        name="level_one_near",
    )(leaf_maps)
    y_33 = swapped(o_33, "box")
    y_32 = swapped(o_31, "box")
    core = here % 2
    modes = lax.dynamic_slice(mode_ids.reshape(-1, 2), (0, core), (16, 1)).reshape(16)
    lanes = jnp.arange(planes, dtype=jnp.int32)
    z_index = jnp.concatenate([here * planes + lanes, (here + 1 - 2 * core) * planes + lanes])
    cas = cas_table(modes, z_index, NZ).reshape(-1)
    line = (boxes * rhs, points)
    pair = pltpu.VMEM((2 * face, face), BF16)
    o_11, o_13, near_data, far_data = pl.pallas_call(
        sums_kernel,
        out_shape=[square, square, rows, rows],
        in_specs=[pl.BlockSpec(memory_space=pltpu.SMEM)] + [ANY] * 6,
        out_specs=[ANY] * 2 + vmem_specs(2),
        scratch_shapes=[
            pltpu.VMEM((2, 7, *line), F32),
            pltpu.VMEM((2, 7, *line), F32),
            pltpu.VMEM((2, *line), F32),
            pltpu.VMEM(line, F32),
            pltpu.VMEM(line, F32),
            pltpu.SemaphoreType.DMA((3, 7)),
            pltpu.SemaphoreType.DMA((3, 7)),
        ]
        + [full] * 11
        + [left, right, right, pair, pair, pair, pair]
        + [pltpu.VMEM((planes, *line), F32)] * 2
        + [pltpu.SemaphoreType.DMA((13,))],
        compiler_params=pltpu.CompilerParams(
            vmem_limit_bytes=VMEM_LIMIT, collective_id=0, has_side_effects=True
        ),
        cost_estimate=cost(100, 5),
        name="hartley_sums",
    )(
        cas,
        sources.reshape(planes, *line),
        other_sources.reshape(planes, *line),
        leaf_maps,
        inv,
        through,
        near_gain,
    )
    other_data = swapped(near_data, "box")
    out, gain = pl.pallas_call(
        top_kernel,
        out_shape=[jax.ShapeDtypeStruct((face, points), F32), square],
        in_specs=[ANY] * 5,
        out_specs=[ANY] * 2,
        scratch_shapes=[full] * 7
        + [left, left, right, right, short, short, full, pltpu.SemaphoreType.DMA((8,))],
        compiler_params=pltpu.CompilerParams(vmem_limit_bytes=LESS_VMEM),
        cost_estimate=cost(22, 8),
        name="level_two_gain",
    )(y_33, o_33, o_31, o_13, o_11)
    out, data = pl.pallas_call(
        last_kernel,
        out_shape=[jax.ShapeDtypeStruct((face, points), F32), rows],
        in_specs=vmem_specs(6) + [ANY],
        out_specs=[ANY] + vmem_specs(1),
        scratch_shapes=[full, left, right, pltpu.SemaphoreType.DMA((2,))],
        input_output_aliases={6: 0},
        compiler_params=pltpu.CompilerParams(vmem_limit_bytes=LAST_VMEM),
        cost_estimate=cost(4, 5),
        name="level_two_rows",
    )(y_32, gain, y_33, near_data, far_data, other_data, out)
    return (out[None, None], data[None, None])


def solution(mesh):
    placed = (P("gz", "box", None, None), P("gz", "box", None, None), P())
    return jax.shard_map(
        local,
        mesh=mesh,
        in_specs=placed,
        out_specs=(P("gz", "box", None, None), P("gz", "box", None, None)),
        check_vma=False,
    )
```

```python
import jax
import jax.numpy as jnp
from jax import lax
from jax.experimental import pallas as pl
from jax.experimental.pallas import tpu as pltpu
from jax.sharding import PartitionSpec as P

NZ = 512
MESH = pl.DeviceIdType.MESH
F32 = jnp.float32
BF16 = jnp.bfloat16
HALF = 256
FINE = 3.6e-9
VMEM_LIMIT = 60 * 1024 * 1024
JOINT_VMEM = 60 * 1024 * 1024
LAST_VMEM = 60 * 1024 * 1024


def split(value):
    high = value.astype(BF16)
    return high, (value - high.astype(F32)).astype(BF16)


def put_left(ref, start, value):
    face = value.shape[1]
    high, low = split(value)
    rows = pl.ds(start, value.shape[0])
    ref[rows, 0:face] = high
    ref[rows, face : 2 * face] = high
    ref[rows, 2 * face : 3 * face] = low


def put_right(ref, start, value):
    face = ref.shape[0] // 3
    high, low = split(value)
    count = value.shape[0]
    ref[pl.ds(start, count), :] = high
    ref[pl.ds(face + start, count), :] = low
    ref[pl.ds(2 * face + start, count), :] = high


def fill(put, ref, source):
    for start in range(0, source.shape[0], HALF):
        put(ref, start, source[start : start + HALF, :])


def product(left, right, start):
    return jnp.dot(left[start : start + HALF, :], right[...], preferred_element_type=F32)


def halves(face):
    return range(0, face, HALF)


def eye_rows(start, face):
    row = lax.broadcasted_iota(jnp.int32, (HALF, face), 0) + start
    col = lax.broadcasted_iota(jnp.int32, (HALF, face), 1)
    return jnp.where(row == col, 1.0, 0.0).astype(F32)


def chunk_sum(part):
    return jnp.sum(part.reshape(-1, 8, part.shape[1]), axis=0)


def invert(k_left, total, power, rough, spare):
    face = total.shape[0]

    def raise_power():
        parts = [
            jnp.dot(power[s : s + HALF, :], power[...], preferred_element_type=F32)
            for s in halves(face)
        ]
        for s, part in zip(halves(face), parts):
            power[s : s + HALF, :] = part.astype(BF16)

    def gather():
        for s in halves(face):
            rough[s : s + HALF, :] = total[s : s + HALF, :].astype(BF16)
        for s in halves(face):
            total[s : s + HALF, :] += jnp.dot(
                rough[s : s + HALF, :], power[...], preferred_element_type=F32
            )

    raise_power()
    for _ in range(3):
        gather()
        raise_power()
    gather()
    for s in halves(face):
        rough[s : s + HALF, :] = total[s : s + HALF, :].astype(BF16)
    first = jnp.zeros((8, face), F32)
    for s in halves(face):
        part = jnp.dot(
            k_left[s : s + HALF, 0:face], rough[...], preferred_element_type=F32
        ) + jnp.dot(
            k_left[s : s + HALF, 2 * face : 3 * face], rough[...], preferred_element_type=F32
        )
        part = part - rough[s : s + HALF, :].astype(F32) + eye_rows(s, face)
        spare[s : s + HALF, :] = part
        power[s : s + HALF, :] = part.astype(BF16)
        first += chunk_sum(part * part)
    second = jnp.zeros((8, face), F32)
    for s in halves(face):
        part = jnp.dot(power[s : s + HALF, :], power[...], preferred_element_type=F32)
        second += chunk_sum(part * part)
        spare[s : s + HALF, :] += part
    for s in halves(face):
        power[s : s + HALF, :] = spare[s : s + HALF, :].astype(BF16)
    for s in halves(face):
        total[s : s + HALF, :] = rough[s : s + HALF, :].astype(F32) + jnp.dot(
            rough[s : s + HALF, :], power[...], preferred_element_type=F32
        )
    return first, second


def poor(first, second):
    first, second = jnp.sum(first), jnp.sum(second)
    return jnp.logical_not((first < 0.25) & (first * second < FINE))


def careful(k_left, total, left, right, spare):
    face = total.shape[0]
    for s in halves(face):
        kept = k_left[s : s + HALF, 0:face].astype(F32)
        kept += k_left[s : s + HALF, 2 * face : 3 * face].astype(F32)
        spare[s : s + HALF, :] = kept
        total[s : s + HALF, :] = kept + eye_rows(s, face)

    def raise_power():
        fill(put_left, left, spare)
        fill(put_right, right, spare)
        size = 0.0
        for s in halves(face):
            part = product(left, right, s)
            spare[s : s + HALF, :] = part
            size += jnp.sum(part * part)
        return size

    def squaring(state):
        count, _ = state
        fill(put_left, left, total)
        fill(put_right, right, spare)
        for s in halves(face):
            total[s : s + HALF, :] += product(left, right, s)
        return count + 1, raise_power()

    lax.while_loop(
        lambda state: (state[1] > 1e-15) & (state[0] < 48),
        squaring,
        (jnp.int32(0), raise_power()),
    )

    def newton(state):
        count, last, _ = state
        fill(put_right, right, total)
        size = 0.0
        for s in halves(face):
            part = product(k_left, right, s) - total[s : s + HALF, :] + eye_rows(s, face)
            spare[s : s + HALF, :] = part
            size += jnp.sum(part * part)
        better = size < 0.25 * last

        @pl.when(better)
        def _():
            fill(put_left, left, total)
            fill(put_right, right, spare)
            for s in halves(face):
                total[s : s + HALF, :] += product(left, right, s)

        return count + 1, size, better

    lax.while_loop(
        lambda state: state[2] & (state[0] < 4),
        newton,
        (jnp.int32(0), jnp.float32(1.0), jnp.bool_(True)),
    )


def fetcher(maps, sems, face):
    def fetch(slot, leaf, row, col, dst):
        copy = pltpu.make_async_copy(
            maps.at[
                0,
                leaf,
                pl.ds(pl.multiple_of(row * face, face), face),
                pl.ds(pl.multiple_of(col * face, face), face),
            ],
            dst,
            sems.at[slot],
        )
        copy.start()
        return copy

    return fetch


def started(src, dst, sem):
    copy = pltpu.make_async_copy(src, dst, sem)
    copy.start()
    return copy


def cas_rows(mode_ids, planes, shape):
    here = lax.axis_index("gz")
    core = here % 2
    row = lax.broadcasted_iota(jnp.int32, shape, 0)
    col = lax.broadcasted_iota(jnp.int32, shape, 1)
    mode = jnp.zeros(shape, jnp.int32)
    for slot in range(shape[0]):
        mode = jnp.where(row == slot, mode_ids[2 * slot + core], mode)
    start = jnp.where(col < planes, here * planes, (here - 2 * core) * planes)
    phase = mode * (start + col) & (NZ - 1)
    angle = phase.astype(F32) * (2.0 * jnp.pi / NZ)
    return (jnp.cos(angle) + jnp.sin(angle)) / NZ**0.5


def near_kernel(mode_ids, maps, cas, o_33_out, gain_out, inv_out, through_out, *scratch):
    a_33, b_33, b_32, b_23, b_22, gain, inv, through = scratch[:8]
    l_one, l_two, k_left, r_one, r_two, power, rough, spare, sems = scratch[8:]
    face = a_33.shape[0]
    far = lax.axis_index("box") % 2
    near = 1 - far
    fetch = fetcher(maps, sems, face)
    copies = [
        fetch(0, far, near, near, a_33),
        fetch(1, near, far, far, b_33),
        fetch(2, near, far, near, b_32),
        fetch(3, near, near, far, b_23),
        fetch(4, near, near, near, b_22),
    ]
    cas[...] = cas_rows(mode_ids, NZ // lax.axis_size("gz"), cas.shape)
    copies[0].wait()
    fill(put_left, l_one, a_33)
    copies[1].wait()
    fill(put_right, r_one, b_33)
    for s in halves(face):
        part = product(l_one, r_one, s)
        put_left(k_left, s, part)
        power[s : s + HALF, :] = part.astype(BF16)
        inv[s : s + HALF, :] = part + eye_rows(s, face)
    copies[2].wait()
    fill(put_right, r_one, b_32)
    for s in halves(face):
        part = product(l_one, r_one, s)
        through[s : s + HALF, :] = part
        put_right(r_two, s, part)
    outs = [started(through, through_out, sems.at[5])]
    first, second = invert(k_left, inv, power, rough, spare)

    @pl.when(poor(first, second))
    def _():
        careful(k_left, inv, l_one, r_one, spare)

    outs.append(started(inv, inv_out, sems.at[6]))
    copies[3].wait()
    fill(put_left, l_one, b_23)
    fill(put_right, r_one, inv)
    for s in halves(face):
        part = product(l_one, r_one, s)
        gain[s : s + HALF, :] = part
        put_left(l_two, s, part)
    outs.append(started(gain, gain_out, sems.at[7]))
    copies[4].wait()
    for s in halves(face):
        b_22[s : s + HALF, :] += product(l_two, r_two, s)
    outs.append(started(b_22, o_33_out, sems.at[8]))
    for copy in outs:
        copy.wait()


def keep_pair(highs, lows, start, value):
    high, low = split(value)
    highs[start : start + value.shape[0], :] = high
    lows[start : start + value.shape[0], :] = low


def rows_times(rows, highs, lows):
    r_high, r_low = split(rows)

    def dot(left, right):
        return lax.dot_general(
            left, right, (((1,), (1,)), ((), ())), preferred_element_type=F32
        )

    return dot(r_high, highs[...]) + (dot(r_low, highs[...]) + dot(r_high, lows[...]))


def last_kernel(norms, data_in, *refs):
    y_32_in, gain_in, own_in, *rest, out, data = refs[:13]
    y_32, gain, own, y_33, o_33, o_31, o_13, o_11, near_data, far_data, beyond = refs[13:24]
    k_left, left, right, inv, other, sems = refs[24:]
    face = gain.shape[0]
    far = lax.axis_index("box") % 2
    scale = (2.0 * face) ** 0.5
    copies = [
        started(src, dst, sems.at[slot])
        for slot, (src, dst) in enumerate(((gain_in, gain), (y_32_in, y_32)))
    ]
    data[...] = data_in[...]
    bad = poor(norms[0:8, :], norms[8:16, :])
    own_cols = pl.ds(pl.multiple_of(far * face, face), face)

    @pl.when(jnp.logical_not(bad))
    def _():
        started(own_in, out.at[:, own_cols], sems.at[8])

    for copy in copies:
        copy.wait()

    @pl.when(bad)
    def _():
        held = (y_33, o_33, o_31, o_13, o_11, near_data, far_data, beyond)
        for slot, (src, dst) in enumerate(zip(rest, held)):
            started(src, dst, sems.at[slot]).wait()
        fill(put_left, left, y_33)
        fill(put_right, right, o_33)
        for s in halves(face):
            put_left(k_left, s, product(left, right, s))
        careful(k_left, inv, left, right, other)
        fill(put_left, left, o_13)
        fill(put_right, right, inv)
        for s in halves(face):
            gain[s : s + HALF, :] = product(left, right, s)
        fill(put_left, left, y_33)
        fill(put_right, right, o_31)
        for s in halves(face):
            other[s : s + HALF, :] = product(left, right, s)
        fill(put_left, left, gain)
        fill(put_right, right, other)
        for s in halves(face):
            own[s : s + HALF, :] = (o_11[s : s + HALF, :] + product(left, right, s)) * scale
        jump = rows_times(near_data[...], *split(y_33[...])) - beyond[...]
        data[...] = far_data[...] + rows_times(jump, *split(gain[...]))
        started(own, out.at[:, own_cols], sems.at[8])

    copies = [pltpu.make_async_copy(own, out.at[:, own_cols], sems.at[8])]
    fill(put_left, left, gain)
    fill(put_right, right, y_32)
    other_cols = pl.ds(pl.multiple_of((1 - far) * face, face), face)
    for s in halves(face):
        rows = slice(s, s + HALF)
        other[rows, :] = product(left, right, s) * -scale
        copies.append(started(other.at[rows, :], out.at[rows, other_cols], sems.at[1 + s // HALF]))
    for copy in copies:
        copy.wait()


def joint_kernel(
    cas, own_in, maps, inv_in, through_in, near_gain_in, o_33_in, *refs
):
    norms, data, y_32, gain_out, own_out, y_33_out, o_31_out, o_13_out, o_11_out = refs[:9]
    near_out, far_out, beyond_out = refs[9:12]
    scratch = refs[12:]
    sent, got, mine, side_sent, side_got, send_sem, recv_sem = scratch[:7]
    near_data, far_data, beyond = scratch[7:10]
    a_13, b_33, b_32, a_11, a_31, a_33, inv, through, near_gain, gain, o_13 = scratch[10:21]
    o_33, o_31, y_33, total, spare = scratch[21:26]
    left, r_one, r_two, l_two, k_left, power, rough = scratch[26:33]
    near_high, near_low, far_high, far_low, own, other, sems = scratch[33:]
    face = inv.shape[0]
    far = lax.axis_index("box") % 2
    near = 1 - far
    fetch = fetcher(maps, sems, face)
    planes_in = started(own_in, own, sems.at[11])
    in_33 = started(o_33_in, o_33, sems.at[13])
    gain_in = started(near_gain_in, near_gain, sems.at[8])
    in_31 = fetch(4, far, near, far, a_31)
    copies_in = [
        fetch(0, far, far, near, a_13),
        fetch(1, near, far, far, b_33),
        fetch(2, near, far, near, b_32),
        started(inv_in, inv, sems.at[3]),
        fetch(5, far, far, far, a_11),
        started(through_in, through, sems.at[6]),
        fetch(7, far, near, near, a_33),
    ]
    here = lax.axis_index("gz")
    core, z, x = here % 2, here // 2 % 8, here // 16

    def device(x_at, z_at, core_at=core):
        return {"gz": x_at * 16 + z_at * 2 + core_at}

    ring = (device(x, (z + 1) % 8), device(x, (z + 7) % 8))
    beside = device(1 - x, z)
    place = lax.axis_index("box")
    planes = own.shape[0]
    partner = {"box": place + 1 - 2 * far}
    barrier = pltpu.get_barrier_semaphore()
    sibling = device(x, z, 1 - core)
    for target in (partner, sibling, *ring, beside):
        pl.semaphore_signal(barrier, inc=1, device_id=target, device_id_type=MESH)

    def post(src, dst, slot, target):
        return pltpu.make_async_remote_copy(
            src_ref=src,
            dst_ref=dst,
            send_sem=send_sem.at[2, slot],
            recv_sem=recv_sem.at[2, slot],
            device_id=target,
            device_id_type=MESH,
        )

    side = post(side_sent, side_got, 0, beside)
    first_block = post(o_33_in, y_33, 1, partner)
    second_block = post(o_31, y_32, 2, partner)
    news = post(near_data, beyond, 3, partner)
    swap = post(own_in, other, 4, sibling)
    pl.semaphore_wait(barrier, 5)
    first_block.start()
    swap.start()

    def term(x_to, z_to, store):
        row = x_to * 8 + z_to

        def block(part, carry):
            rows = pl.ds(pl.multiple_of(part * 8, 8), 8)
            total = cas[row, 0] * own[0, rows, :]
            for k in range(1, planes):
                total += cas[row, k] * own[k, rows, :]
            for k in range(planes):
                total += cas[row, planes + k] * other[k, rows, :]
            store(rows, total)
            return carry

        lax.fori_loop(0, own.shape[1] // 8, block, 0)

    def message(way, index):
        return pltpu.make_async_remote_copy(
            src_ref=sent.at[way, index],
            dst_ref=got.at[way, index],
            send_sem=send_sem.at[way, index],
            recv_sem=recv_sem.at[way, index],
            device_id=ring[way],
            device_id_type=MESH,
        )

    copies_out = []

    def send_second():
        gain_in.wait()
        in_31.wait()
        fill(put_left, left, near_gain)
        fill(put_right, r_one, a_31)
        for s in halves(face):
            o_31[s : s + HALF, :] = -product(left, r_one, s)
        second_block.start()
        copies_out.append(started(o_31, o_31_out, sems.at[8]))

    def work_0():
        copies_in[0].wait()
        fill(put_left, left, a_13)
        copies_in[1].wait()
        fill(put_right, r_two, b_33)
        for s in halves(face):
            gain[s : s + HALF, :] = product(left, r_two, s)

    def work_1():
        copies_in[2].wait()
        fill(put_right, r_two, b_32)
        for s in halves(face):
            o_13[s : s + HALF, :] = -product(left, r_two, s)

    def work_2():
        copies_in[3].wait()
        fill(put_left, left, gain)
        fill(put_right, r_two, inv)
        for s in halves(face):
            gain[s : s + HALF, :] = product(left, r_two, s)

    def work_3():
        fill(put_left, left, gain)
        copies_in[4].wait()
        for s in halves(face):
            a_11[s : s + HALF, :] += product(left, r_one, s)
        copies_out.append(started(a_11, o_11_out, sems.at[9]))

    def work_4():
        copies_in[5].wait()
        fill(put_right, r_two, through)
        for s in halves(face):
            o_13[s : s + HALF, :] -= product(left, r_two, s)
        copies_out.append(started(o_13, o_13_out, sems.at[10]))

    def work_5():
        copies_in[6].wait()
        for s in halves(face):
            rows = slice(s, s + HALF)
            keep_pair(far_high, far_low, s, a_33[rows, :])
            keep_pair(far_high, far_low, face + s, a_13[rows, :])
            keep_pair(near_high, near_low, s, near_gain[rows, :])
            keep_pair(near_high, near_low, face + s, gain[rows, :])

    send_second()
    work_0()
    planes_in.wait()
    swap.wait_recv()
    work = (work_1, work_2, work_3, work_4, work_5)
    copies = [[message(way, index) for index in range(7)] for way in range(2)]
    for index in range(7):
        step = (index + 3) // 2
        first = index % 2 == 0
        for way in range(2):
            x_to = way if first else 1 - way
            z_to = (z + (5 - step)) % 8 if way == 0 else (z + 8 - (5 - step)) % 8

            def store(rows, total, way=way, index=index):
                sent[way, index, rows, :] = total

            term(x_to, z_to, store)
            if index >= 2:
                copies[way][index - 2].wait_recv()
                sent[way, index] += got[way, index - 2]
            copies[way][index].start()
        if index < len(work):
            work[index]()
    for x_to in range(2):

        def store(rows, total, x_to=x_to):
            mine[x_to, rows, :] = total

        term(x_to, z, store)
    for index in (5, 6):
        for way in range(2):
            copies[way][index].wait_recv()
    away = 1 - x
    side_sent[...] = mine[away] + (got[0, 6 - away] + got[1, 5 + away])
    side.start()
    mine[x] += got[0, 6 - x] + got[1, 5 + x]
    first_block.wait_recv()
    copies_out.append(started(y_33, y_33_out, sems.at[0]))
    in_33.wait()
    fill(put_left, l_two, y_33)
    fill(put_right, r_one, o_33)
    for s in halves(face):
        part = product(l_two, r_one, s)
        put_left(k_left, s, part)
        power[s : s + HALF, :] = part.astype(BF16)
        total[s : s + HALF, :] = part + eye_rows(s, face)
    side.wait_recv()
    mine[x] += side_got[...]
    rhs = near_data.shape[0]

    def info(leaf, side):
        return mine[
            x,
            pl.ds(pl.multiple_of(leaf * rhs, rhs), rhs),
            pl.ds(pl.multiple_of(side * face, face), face),
        ]

    known = rows_times(info(near, far), far_high, far_low)
    jump = info(far, near) - known[:, 0:face]
    moved = rows_times(jump, near_high, near_low)
    near_data[...] = info(near, near) - moved[:, 0:face]
    news.start()
    far_data[...] = info(far, far) + moved[:, face : 2 * face] - known[:, face : 2 * face]
    copies_out.append(started(near_data, near_out, sems.at[1]))
    copies_out.append(started(far_data, far_out, sems.at[2]))
    fill(put_right, r_one, o_31)
    for s in halves(face):
        put_right(r_two, s, product(l_two, r_one, s))
    norms[0:8, :], norms[8:16, :] = invert(k_left, total, power, rough, spare)
    fill(put_left, left, o_13)
    fill(put_right, r_one, total)
    for s in halves(face):
        part = product(left, r_one, s)
        gain[s : s + HALF, :] = part
        put_left(k_left, s, part)
    copies_out.append(started(gain, gain_out, sems.at[4]))
    scale = (2.0 * face) ** 0.5
    for s in halves(face):
        total[s : s + HALF, :] = (a_11[s : s + HALF, :] + product(k_left, r_two, s)) * scale
    copies_out.append(started(total, own_out, sems.at[5]))
    news.wait_recv()
    copies_out.append(started(beyond, beyond_out, sems.at[3]))
    jump = rows_times(near_data[...], l_two.at[:, 0:face], l_two.at[:, 2 * face :])
    jump -= beyond[...]
    data[...] = far_data[...] + rows_times(
        jump, k_left.at[:, 0:face], k_left.at[:, 2 * face :]
    )
    for way in range(2):
        for index in range(7):
            copies[way][index].wait_send()
    for copy in (side, first_block, second_block, news, swap):
        copy.wait_send()
    for copy in copies_out:
        copy.wait()
    second_block.wait_recv()


def vmem_specs(count):
    return [pl.BlockSpec(memory_space=pltpu.VMEM)] * count


ANY = pl.BlockSpec(memory_space=pl.ANY)


def local(sources, leaf_maps, mode_ids):
    planes, boxes, rhs, points = sources.shape
    face = points // 2
    square = jax.ShapeDtypeStruct((face, face), F32)
    rows = jax.ShapeDtypeStruct((rhs, face), F32)
    full = pltpu.VMEM((face, face), F32)
    short = pltpu.VMEM((face, face), BF16)
    left = pltpu.VMEM((face, 3 * face), BF16)
    right = pltpu.VMEM((3 * face, face), BF16)
    params = pltpu.CompilerParams(vmem_limit_bytes=VMEM_LIMIT)

    def cost(units, size):
        return pl.CostEstimate(
            flops=units * 2 * face**3, bytes_accessed=size * 4 * face**2, transcendentals=0
        )

    cas, o_33, near_gain, inv, through = pl.pallas_call(
        near_kernel,
        out_shape=[jax.ShapeDtypeStruct((mode_ids.shape[0] // 2, 128), F32)] + [square] * 4,
        in_specs=[pl.BlockSpec(memory_space=pltpu.SMEM), ANY],
        out_specs=vmem_specs(1) + [ANY] * 4,
        scratch_shapes=[full] * 8
        + [left, left, left, right, right, short, short, full, pltpu.SemaphoreType.DMA((9,))],
        compiler_params=params,
        cost_estimate=cost(24, 9),
        name="level_one_near",
    )(mode_ids, leaf_maps)
    line = (boxes * rhs, points)
    pair = pltpu.VMEM((2 * face, face), BF16)
    narrow = pltpu.VMEM((rhs, face), F32)
    whole = jax.ShapeDtypeStruct((face, points), F32)
    norms, data, *made = pl.pallas_call(
        joint_kernel,
        out_shape=[jax.ShapeDtypeStruct((16, face), F32), rows] + [square] * 7 + [rows] * 3,
        in_specs=[pl.BlockSpec(memory_space=pltpu.SMEM)] + [ANY] * 6,
        out_specs=vmem_specs(2) + [ANY] * 10,
        scratch_shapes=[
            pltpu.VMEM((2, 7, *line), F32),
            pltpu.VMEM((2, 7, *line), F32),
            pltpu.VMEM((2, *line), F32),
            pltpu.VMEM(line, F32),
            pltpu.VMEM(line, F32),
            pltpu.SemaphoreType.DMA((3, 7)),
            pltpu.SemaphoreType.DMA((3, 7)),
            narrow,
            narrow,
            narrow,
        ]
        + [full] * 16
        + [left, right, right, left, left, short, short]
        + [pair, pair, pair, pair]
        + [pltpu.VMEM((planes, *line), F32)] * 2
        + [pltpu.SemaphoreType.DMA((16,))],
        compiler_params=pltpu.CompilerParams(
            vmem_limit_bytes=JOINT_VMEM, collective_id=0, has_side_effects=True
        ),
        cost_estimate=cost(100, 20),
        name="exchange_sums_level_two",
    )(
        cas,
        sources.reshape(planes, *line),
        leaf_maps,
        inv,
        through,
        near_gain,
        o_33,
    )
    y_32, gain, own, y_33, o_31, o_13, o_11, near_data, far_data, beyond = made
    out, data = pl.pallas_call(
        last_kernel,
        out_shape=[whole, rows],
        in_specs=vmem_specs(2) + [ANY] * 11,
        out_specs=[ANY] + vmem_specs(1),
        scratch_shapes=[full] * 8
        + [narrow] * 3
        + [left, left, right, full, full, pltpu.SemaphoreType.DMA((9,))],
        compiler_params=pltpu.CompilerParams(vmem_limit_bytes=LAST_VMEM),
        cost_estimate=cost(4, 5),
        name="level_two_rows",
    )(norms, data, y_32, gain, own, y_33, o_33, o_31, o_13, o_11, near_data, far_data, beyond)
    return (out[None, None], data[None, None])


def solution(mesh):
    placed = (P("gz", "box", None, None), P("gz", "box", None, None), P())
    return jax.shard_map(
        local,
        mesh=mesh,
        in_specs=placed,
        out_specs=(P("gz", "box", None, None), P("gz", "box", None, None)),
        check_vma=False,
    )
```

```python
import jax
import jax.numpy as jnp
from jax import lax
from jax.experimental import pallas as pl
from jax.experimental.pallas import tpu as pltpu
from jax.sharding import PartitionSpec as P

NZ = 512
MESH = pl.DeviceIdType.MESH
F32 = jnp.float32
BF16 = jnp.bfloat16
HALF = 256
FINE = 3.6e-9
VMEM_LIMIT = 60 * 1024 * 1024
LESS_VMEM = 50 * 1024 * 1024
LAST_VMEM = 28 * 1024 * 1024


def swapped(block, axis):
    count = lax.axis_size(axis)
    route = []
    for low in range(0, count, 2):
        route += [(low, low + 1), (low + 1, low)]
    return lax.ppermute(block, axis, route)


def split(value):
    high = value.astype(BF16)
    return high, (value - high.astype(F32)).astype(BF16)


def put_left(ref, start, value):
    face = value.shape[1]
    high, low = split(value)
    rows = pl.ds(start, value.shape[0])
    ref[rows, 0:face] = high
    ref[rows, face : 2 * face] = high
    ref[rows, 2 * face : 3 * face] = low


def put_right(ref, start, value):
    face = ref.shape[0] // 3
    high, low = split(value)
    count = value.shape[0]
    ref[pl.ds(start, count), :] = high
    ref[pl.ds(face + start, count), :] = low
    ref[pl.ds(2 * face + start, count), :] = high


def fill(put, ref, source):
    for start in range(0, source.shape[0], HALF):
        put(ref, start, source[start : start + HALF, :])


def product(left, right, start):
    return jnp.dot(left[start : start + HALF, :], right[...], preferred_element_type=F32)


def halves(face):
    return range(0, face, HALF)


def eye_rows(start, face):
    row = lax.broadcasted_iota(jnp.int32, (HALF, face), 0) + start
    col = lax.broadcasted_iota(jnp.int32, (HALF, face), 1)
    return jnp.where(row == col, 1.0, 0.0).astype(F32)


def chunk_sum(part):
    return jnp.sum(part.reshape(-1, 8, part.shape[1]), axis=0)


def invert(k_left, total, power, rough, left, right, spare):
    face = total.shape[0]

    def raise_power():
        parts = [
            jnp.dot(power[s : s + HALF, :], power[...], preferred_element_type=F32)
            for s in halves(face)
        ]
        for s, part in zip(halves(face), parts):
            power[s : s + HALF, :] = part.astype(BF16)

    def gather():
        for s in halves(face):
            rough[s : s + HALF, :] = total[s : s + HALF, :].astype(BF16)
        for s in halves(face):
            total[s : s + HALF, :] += jnp.dot(
                rough[s : s + HALF, :], power[...], preferred_element_type=F32
            )

    raise_power()
    for _ in range(3):
        gather()
        raise_power()
    gather()
    for s in halves(face):
        rough[s : s + HALF, :] = total[s : s + HALF, :].astype(BF16)
    first = jnp.zeros((8, face), F32)
    for s in halves(face):
        part = jnp.dot(
            k_left[s : s + HALF, 0:face], rough[...], preferred_element_type=F32
        ) + jnp.dot(
            k_left[s : s + HALF, 2 * face : 3 * face], rough[...], preferred_element_type=F32
        )
        part = part - rough[s : s + HALF, :].astype(F32) + eye_rows(s, face)
        spare[s : s + HALF, :] = part
        power[s : s + HALF, :] = part.astype(BF16)
        first += chunk_sum(part * part)
    second = jnp.zeros((8, face), F32)
    for s in halves(face):
        part = jnp.dot(power[s : s + HALF, :], power[...], preferred_element_type=F32)
        second += chunk_sum(part * part)
        spare[s : s + HALF, :] += part
    for s in halves(face):
        power[s : s + HALF, :] = spare[s : s + HALF, :].astype(BF16)
    for s in halves(face):
        total[s : s + HALF, :] = rough[s : s + HALF, :].astype(F32) + jnp.dot(
            rough[s : s + HALF, :], power[...], preferred_element_type=F32
        )
    first, second = jnp.sum(first), jnp.sum(second)

    @pl.when(jnp.logical_not((first < 0.25) & (first * second < FINE)))
    def _():
        careful(k_left, total, left, right, spare)


def careful(k_left, total, left, right, spare):
    face = total.shape[0]
    for s in halves(face):
        kept = k_left[s : s + HALF, 0:face].astype(F32)
        kept += k_left[s : s + HALF, 2 * face : 3 * face].astype(F32)
        spare[s : s + HALF, :] = kept
        total[s : s + HALF, :] = kept + eye_rows(s, face)

    def raise_power():
        fill(put_left, left, spare)
        fill(put_right, right, spare)
        size = 0.0
        for s in halves(face):
            part = product(left, right, s)
            spare[s : s + HALF, :] = part
            size += jnp.sum(part * part)
        return size

    def squaring(state):
        count, _ = state
        fill(put_left, left, total)
        fill(put_right, right, spare)
        for s in halves(face):
            total[s : s + HALF, :] += product(left, right, s)
        return count + 1, raise_power()

    lax.while_loop(
        lambda state: (state[1] > 1e-15) & (state[0] < 48),
        squaring,
        (jnp.int32(0), raise_power()),
    )

    def newton(state):
        count, last, _ = state
        fill(put_right, right, total)
        size = 0.0
        for s in halves(face):
            part = product(k_left, right, s) - total[s : s + HALF, :] + eye_rows(s, face)
            spare[s : s + HALF, :] = part
            size += jnp.sum(part * part)
        better = size < 0.25 * last

        @pl.when(better)
        def _():
            fill(put_left, left, total)
            fill(put_right, right, spare)
            for s in halves(face):
                total[s : s + HALF, :] += product(left, right, s)

        return count + 1, size, better

    lax.while_loop(
        lambda state: state[2] & (state[0] < 4),
        newton,
        (jnp.int32(0), jnp.float32(1.0), jnp.bool_(True)),
    )


def fetcher(maps, sems, face):
    def fetch(slot, leaf, row, col, dst):
        copy = pltpu.make_async_copy(
            maps.at[
                0,
                leaf,
                pl.ds(pl.multiple_of(row * face, face), face),
                pl.ds(pl.multiple_of(col * face, face), face),
            ],
            dst,
            sems.at[slot],
        )
        copy.start()
        return copy

    return fetch


def started(src, dst, sem):
    copy = pltpu.make_async_copy(src, dst, sem)
    copy.start()
    return copy


def cas_rows(mode_ids, planes, shape):
    here = lax.axis_index("gz")
    core = here % 2
    row = lax.broadcasted_iota(jnp.int32, shape, 0)
    col = lax.broadcasted_iota(jnp.int32, shape, 1)
    mode = jnp.zeros(shape, jnp.int32)
    for slot in range(shape[0]):
        mode = jnp.where(row == slot, mode_ids[2 * slot + core], mode)
    start = jnp.where(col < planes, here * planes, (here - 2 * core) * planes)
    phase = mode * (start + col) & (NZ - 1)
    quarter = (phase + NZ // 8) // (NZ // 4)
    angle = (phase - quarter * (NZ // 4)).astype(F32) * (2.0 * jnp.pi / NZ)
    power = angle * angle
    cosine = jnp.ones(shape, F32)
    sine = jnp.ones(shape, F32)
    for k in (5, 4, 3, 2, 1):
        cosine = 1.0 - power * cosine * (1.0 / ((2 * k - 1) * (2 * k)))
        sine = 1.0 - power * sine * (1.0 / ((2 * k) * (2 * k + 1)))
    sine = sine * angle
    value = jnp.where(quarter % 2 == 0, cosine + sine, cosine - sine)
    return jnp.where(quarter % 4 < 2, value, -value) * (1.0 / NZ**0.5)


def near_kernel(
    mode_ids, maps, cas, o_33_out, o_31_out, gain_out, inv_out, through_out, *scratch
):
    a_33, b_33, b_32, b_23, b_22, a_31, gain, inv, through = scratch[:9]
    l_one, l_two, k_left, r_one, r_two, power, rough, spare, sems = scratch[9:]
    face = a_33.shape[0]
    far = lax.axis_index("box") % 2
    near = 1 - far
    fetch = fetcher(maps, sems, face)
    copies = [
        fetch(0, far, near, near, a_33),
        fetch(1, near, far, far, b_33),
    ]
    cas[...] = cas_rows(mode_ids, NZ // lax.axis_size("gz"), cas.shape)
    copies[0].wait()
    fill(put_left, l_one, a_33)
    copies[1].wait()
    copies += [
        fetch(2, near, far, near, b_32),
        fetch(3, near, near, far, b_23),
        fetch(4, near, near, near, b_22),
        fetch(5, far, near, far, a_31),
    ]
    fill(put_right, r_one, b_33)
    for s in halves(face):
        part = product(l_one, r_one, s)
        put_left(k_left, s, part)
        power[s : s + HALF, :] = part.astype(BF16)
        inv[s : s + HALF, :] = part + eye_rows(s, face)
    copies[2].wait()
    fill(put_right, r_one, b_32)
    for s in halves(face):
        part = product(l_one, r_one, s)
        through[s : s + HALF, :] = part
        put_right(r_two, s, part)
    outs = [started(through, through_out, sems.at[6])]
    invert(k_left, inv, power, rough, l_one, r_one, spare)
    outs.append(started(inv, inv_out, sems.at[7]))
    copies[3].wait()
    fill(put_left, l_one, b_23)
    fill(put_right, r_one, inv)
    for s in halves(face):
        part = product(l_one, r_one, s)
        gain[s : s + HALF, :] = part
        put_left(l_two, s, part)
    outs.append(started(gain, gain_out, sems.at[8]))
    copies[4].wait()
    for s in halves(face):
        b_22[s : s + HALF, :] += product(l_two, r_two, s)
    outs.append(started(b_22, o_33_out, sems.at[9]))
    copies[5].wait()
    fill(put_right, r_one, a_31)
    for s in halves(face):
        a_31[s : s + HALF, :] = -product(l_two, r_one, s)
    outs.append(started(a_31, o_31_out, sems.at[10]))
    for copy in outs:
        copy.wait()


def keep_pair(highs, lows, start, value):
    high, low = split(value)
    highs[start : start + value.shape[0], :] = high
    lows[start : start + value.shape[0], :] = low


def rows_times(rows, highs, lows):
    r_high, r_low = split(rows)

    def dot(left, right):
        return lax.dot_general(
            left, right, (((1,), (1,)), ((), ())), preferred_element_type=F32
        )

    return dot(r_high, highs[...]) + (dot(r_low, highs[...]) + dot(r_high, lows[...]))


def top_kernel(y_33, o_33, o_31_in, o_13_in, o_11_in, out, gain_out, *scratch):
    o_31, o_13, o_11, gain, inv = scratch[:5]
    l_one, k_left, r_one, r_two, power, rough, spare, sems = scratch[5:]
    face = y_33.shape[0]
    far = lax.axis_index("box") % 2
    copies = [
        started(src, dst, sems.at[slot])
        for slot, (src, dst) in enumerate(((o_31_in, o_31), (o_13_in, o_13), (o_11_in, o_11)))
    ]
    fill(put_left, l_one, y_33)
    fill(put_right, r_one, o_33)
    for s in halves(face):
        part = product(l_one, r_one, s)
        put_left(k_left, s, part)
        power[s : s + HALF, :] = part.astype(BF16)
        inv[s : s + HALF, :] = part + eye_rows(s, face)
    copies[0].wait()
    fill(put_right, r_one, o_31)
    for s in halves(face):
        put_right(r_two, s, product(l_one, r_one, s))
    invert(k_left, inv, power, rough, l_one, r_one, spare)
    copies[1].wait()
    fill(put_left, l_one, o_13)
    fill(put_right, r_one, inv)
    for s in halves(face):
        part = product(l_one, r_one, s)
        gain[s : s + HALF, :] = part
        put_left(k_left, s, part)
    last = [started(gain, gain_out, sems.at[5])]
    scale = (2.0 * face) ** 0.5
    copies[2].wait()
    for s in halves(face):
        o_11[s : s + HALF, :] = (o_11[s : s + HALF, :] + product(k_left, r_two, s)) * scale
        last.append(
            started(
                o_11.at[s : s + HALF, :],
                out.at[s : s + HALF, pl.ds(pl.multiple_of(far * face, face), face)],
                sems.at[6 + s // HALF],
            )
        )
    for copy in last:
        copy.wait()


def last_kernel(
    y_32, gain, y_33, near_data, far_data, other_data, _, out, data, other, left, right, sems
):
    face = gain.shape[0]
    near = 1 - lax.axis_index("box") % 2
    scale = (2.0 * face) ** 0.5
    fill(put_left, left, gain)
    fill(put_right, right, y_32)
    copies = []
    for s in halves(face):
        other[s : s + HALF, :] = product(left, right, s) * -scale
        copies.append(
            started(
                other.at[s : s + HALF, :],
                out.at[s : s + HALF, pl.ds(pl.multiple_of(near * face, face), face)],
                sems.at[s // HALF],
            )
        )
    jump = rows_times(near_data[...], *split(y_33[...])) - other_data[...]
    data[...] = far_data[...] + rows_times(jump, *split(gain[...]))
    for copy in copies:
        copy.wait()


def sums_kernel(
    cas, own_in, other_in, maps, inv_in, through_in, near_gain_in, o_11_out, o_13_out, *scratch
):
    near_data, far_data, sent, got, mine, side_sent, side_got, send_sem, recv_sem = scratch[:9]
    a_13, b_33, b_32, a_11, a_31, a_33, inv, through, near_gain, gain, o_13 = scratch[9:20]
    left, r_one, r_two, near_high, near_low, far_high, far_low, own, other, sems = scratch[20:]
    face = inv.shape[0]
    far = lax.axis_index("box") % 2
    near = 1 - far
    fetch = fetcher(maps, sems, face)
    planes_in = (started(own_in, own, sems.at[11]), started(other_in, other, sems.at[12]))
    here = lax.axis_index("gz")
    core, z, x = here % 2, here // 2 % 8, here // 16

    def device(x_at, z_at):
        return {"gz": x_at * 16 + z_at * 2 + core}

    ring = (device(x, (z + 1) % 8), device(x, (z + 7) % 8))
    beside = device(1 - x, z)
    barrier = pltpu.get_barrier_semaphore()
    for target in (*ring, beside):
        pl.semaphore_signal(barrier, inc=1, device_id=target, device_id_type=MESH)
    for copy in planes_in:
        copy.wait()
    copies_in = [
        fetch(0, far, far, near, a_13),
        fetch(1, near, far, far, b_33),
        fetch(2, near, far, near, b_32),
        started(inv_in, inv, sems.at[3]),
        fetch(4, far, near, far, a_31),
        fetch(5, far, far, far, a_11),
        started(through_in, through, sems.at[6]),
        fetch(7, far, near, near, a_33),
        started(near_gain_in, near_gain, sems.at[8]),
    ]
    planes = own.shape[0]

    def term(x_to, z_to, store):
        row = x_to * 8 + z_to

        def block(part, carry):
            rows = pl.ds(pl.multiple_of(part * 8, 8), 8)
            total = cas[row, 0] * own[0, rows, :]
            for k in range(1, planes):
                total += cas[row, k] * own[k, rows, :]
            for k in range(planes):
                total += cas[row, planes + k] * other[k, rows, :]
            store(rows, total)
            return carry

        lax.fori_loop(0, own.shape[1] // 8, block, 0)

    def message(way, index):
        return pltpu.make_async_remote_copy(
            src_ref=sent.at[way, index],
            dst_ref=got.at[way, index],
            send_sem=send_sem.at[way, index],
            recv_sem=recv_sem.at[way, index],
            device_id=ring[way],
            device_id_type=MESH,
        )

    copies_out = []

    def work_0():
        copies_in[0].wait()
        fill(put_left, left, a_13)
        copies_in[1].wait()
        fill(put_right, r_one, b_33)
        for s in halves(face):
            gain[s : s + HALF, :] = product(left, r_one, s)

    def work_1():
        copies_in[2].wait()
        fill(put_right, r_two, b_32)
        for s in halves(face):
            o_13[s : s + HALF, :] = -product(left, r_two, s)

    def work_2():
        copies_in[3].wait()
        fill(put_left, left, gain)
        fill(put_right, r_one, inv)
        for s in halves(face):
            gain[s : s + HALF, :] = product(left, r_one, s)

    def work_3():
        fill(put_left, left, gain)
        copies_in[4].wait()
        copies_in[5].wait()
        fill(put_right, r_one, a_31)
        for s in halves(face):
            a_11[s : s + HALF, :] += product(left, r_one, s)
        copies_out.append(started(a_11, o_11_out, sems.at[9]))

    def work_4():
        copies_in[6].wait()
        fill(put_right, r_two, through)
        for s in halves(face):
            o_13[s : s + HALF, :] -= product(left, r_two, s)
        copies_out.append(started(o_13, o_13_out, sems.at[10]))

    def work_5():
        copies_in[7].wait()
        copies_in[8].wait()
        for s in halves(face):
            rows = slice(s, s + HALF)
            keep_pair(far_high, far_low, s, a_33[rows, :])
            keep_pair(far_high, far_low, face + s, a_13[rows, :])
            keep_pair(near_high, near_low, s, near_gain[rows, :])
            keep_pair(near_high, near_low, face + s, gain[rows, :])

    work = (work_0, work_1, work_2, work_3, work_4, work_5, lambda: None)
    copies = [[message(way, index) for index in range(7)] for way in range(2)]
    for index in range(7):
        step = (index + 3) // 2
        first = index % 2 == 0
        for way in range(2):
            x_to = way if first else 1 - way
            z_to = (z + (5 - step)) % 8 if way == 0 else (z + 8 - (5 - step)) % 8

            def store(rows, total, way=way, index=index):
                sent[way, index, rows, :] = total

            term(x_to, z_to, store)
            if index == 0 and way == 0:
                pl.semaphore_wait(barrier, 3)
            if index >= 2:
                copies[way][index - 2].wait_recv()
                sent[way, index] += got[way, index - 2]
            copies[way][index].start()
        work[index]()
    for x_to in range(2):

        def store(rows, total, x_to=x_to):
            mine[x_to, rows, :] = total

        term(x_to, z, store)
    for index in (5, 6):
        for way in range(2):
            copies[way][index].wait_recv()
    away = 1 - x
    side_sent[...] = mine[away] + (got[0, 6 - away] + got[1, 5 + away])
    last = pltpu.make_async_remote_copy(
        src_ref=side_sent,
        dst_ref=side_got,
        send_sem=send_sem.at[2, 0],
        recv_sem=recv_sem.at[2, 0],
        device_id=beside,
        device_id_type=MESH,
    )
    last.start()
    mine[x] += got[0, 6 - x] + got[1, 5 + x]
    last.wait_recv()
    mine[x] += side_got[...]
    rhs = near_data.shape[0]

    def info(leaf, side):
        return mine[
            x,
            pl.ds(pl.multiple_of(leaf * rhs, rhs), rhs),
            pl.ds(pl.multiple_of(side * face, face), face),
        ]

    known = rows_times(info(near, far), far_high, far_low)
    jump = info(far, near) - known[:, 0:face]
    moved = rows_times(jump, near_high, near_low)
    near_data[...] = info(near, near) - moved[:, 0:face]
    far_data[...] = info(far, far) + moved[:, face : 2 * face] - known[:, face : 2 * face]
    for way in range(2):
        for index in range(7):
            copies[way][index].wait_send()
    last.wait_send()
    for copy in copies_out:
        copy.wait()


def vmem_specs(count):
    return [pl.BlockSpec(memory_space=pltpu.VMEM)] * count


ANY = pl.BlockSpec(memory_space=pl.ANY)


def local(sources, leaf_maps, mode_ids):
    planes, boxes, rhs, points = sources.shape
    face = points // 2
    square = jax.ShapeDtypeStruct((face, face), F32)
    rows = jax.ShapeDtypeStruct((rhs, face), F32)
    full = pltpu.VMEM((face, face), F32)
    short = pltpu.VMEM((face, face), BF16)
    left = pltpu.VMEM((face, 3 * face), BF16)
    right = pltpu.VMEM((3 * face, face), BF16)
    params = pltpu.CompilerParams(vmem_limit_bytes=VMEM_LIMIT)

    def cost(units, size):
        return pl.CostEstimate(
            flops=units * 2 * face**3, bytes_accessed=size * 4 * face**2, transcendentals=0
        )

    other_sources = swapped(sources, "gz")
    cas, o_33, o_31, near_gain, inv, through = pl.pallas_call(
        near_kernel,
        out_shape=[jax.ShapeDtypeStruct((mode_ids.shape[0] // 2, 128), F32)] + [square] * 5,
        in_specs=[pl.BlockSpec(memory_space=pltpu.SMEM), ANY],
        out_specs=vmem_specs(1) + [ANY] * 5,
        scratch_shapes=[full] * 9
        + [left, left, left, right, right, short, short, full, pltpu.SemaphoreType.DMA((11,))],
        compiler_params=params,
        cost_estimate=cost(27, 11),
        name="level_one_near",
    )(mode_ids, leaf_maps)
    y_33 = swapped(o_33, "box")
    y_32 = swapped(o_31, "box")
    line = (boxes * rhs, points)
    pair = pltpu.VMEM((2 * face, face), BF16)
    o_11, o_13, near_data, far_data = pl.pallas_call(
        sums_kernel,
        out_shape=[square, square, rows, rows],
        in_specs=[pl.BlockSpec(memory_space=pltpu.SMEM)] + [ANY] * 6,
        out_specs=[ANY] * 2 + vmem_specs(2),
        scratch_shapes=[
            pltpu.VMEM((2, 7, *line), F32),
            pltpu.VMEM((2, 7, *line), F32),
            pltpu.VMEM((2, *line), F32),
            pltpu.VMEM(line, F32),
            pltpu.VMEM(line, F32),
            pltpu.SemaphoreType.DMA((3, 7)),
            pltpu.SemaphoreType.DMA((3, 7)),
        ]
        + [full] * 11
        + [left, right, right, pair, pair, pair, pair]
        + [pltpu.VMEM((planes, *line), F32)] * 2
        + [pltpu.SemaphoreType.DMA((13,))],
        compiler_params=pltpu.CompilerParams(
            vmem_limit_bytes=VMEM_LIMIT, collective_id=0, has_side_effects=True
        ),
        cost_estimate=cost(100, 5),
        name="hartley_sums",
    )(
        cas,
        sources.reshape(planes, *line),
        other_sources.reshape(planes, *line),
        leaf_maps,
        inv,
        through,
        near_gain,
    )
    other_data = swapped(near_data, "box")
    out, gain = pl.pallas_call(
        top_kernel,
        out_shape=[jax.ShapeDtypeStruct((face, points), F32), square],
        in_specs=vmem_specs(2) + [ANY] * 3,
        out_specs=[ANY] * 2,
        scratch_shapes=[full] * 5
        + [left, left, right, right, short, short, full, pltpu.SemaphoreType.DMA((8,))],
        compiler_params=pltpu.CompilerParams(vmem_limit_bytes=LESS_VMEM),
        cost_estimate=cost(22, 8),
        name="level_two_gain",
    )(y_33, o_33, o_31, o_13, o_11)
    out, data = pl.pallas_call(
        last_kernel,
        out_shape=[jax.ShapeDtypeStruct((face, points), F32), rows],
        in_specs=vmem_specs(6) + [ANY],
        out_specs=[ANY] + vmem_specs(1),
        scratch_shapes=[full, left, right, pltpu.SemaphoreType.DMA((2,))],
        input_output_aliases={6: 0},
        compiler_params=pltpu.CompilerParams(vmem_limit_bytes=LAST_VMEM),
        cost_estimate=cost(4, 5),
        name="level_two_rows",
    )(y_32, gain, y_33, near_data, far_data, other_data, out)
    return (out[None, None], data[None, None])


def solution(mesh):
    placed = (P("gz", "box", None, None), P("gz", "box", None, None), P())
    return jax.shard_map(
        local,
        mesh=mesh,
        in_specs=placed,
        out_specs=(P("gz", "box", None, None), P("gz", "box", None, None)),
        check_vma=False,
    )
```

```python
import jax
import jax.numpy as jnp
from jax import lax
from jax.experimental import pallas as pl
from jax.experimental.pallas import tpu as pltpu
from jax.sharding import PartitionSpec as P

NZ = 512
MESH = pl.DeviceIdType.MESH
F32 = jnp.float32
BF16 = jnp.bfloat16
HALF = 256
FINE = 3.6e-9
VMEM_LIMIT = 60 * 1024 * 1024
LESS_VMEM = 50 * 1024 * 1024
LAST_VMEM = 28 * 1024 * 1024


def swapped(block, axis):
    count = lax.axis_size(axis)
    route = []
    for low in range(0, count, 2):
        route += [(low, low + 1), (low + 1, low)]
    return lax.ppermute(block, axis, route)


def split(value):
    high = value.astype(BF16)
    return high, (value - high.astype(F32)).astype(BF16)


def put_left(ref, start, value):
    face = value.shape[1]
    high, low = split(value)
    rows = pl.ds(start, value.shape[0])
    ref[rows, 0:face] = high
    ref[rows, face : 2 * face] = high
    ref[rows, 2 * face : 3 * face] = low


def put_right(ref, start, value):
    face = ref.shape[0] // 3
    high, low = split(value)
    count = value.shape[0]
    ref[pl.ds(start, count), :] = high
    ref[pl.ds(face + start, count), :] = low
    ref[pl.ds(2 * face + start, count), :] = high


def fill(put, ref, source):
    for start in range(0, source.shape[0], HALF):
        put(ref, start, source[start : start + HALF, :])


def product(left, right, start):
    return jnp.dot(left[start : start + HALF, :], right[...], preferred_element_type=F32)


def halves(face):
    return range(0, face, HALF)


def eye_rows(start, face):
    row = lax.broadcasted_iota(jnp.int32, (HALF, face), 0) + start
    col = lax.broadcasted_iota(jnp.int32, (HALF, face), 1)
    return jnp.where(row == col, 1.0, 0.0).astype(F32)


def chunk_sum(part):
    return jnp.sum(part.reshape(-1, 8, part.shape[1]), axis=0)


def invert(k_left, total, power, rough, left, right, spare):
    face = total.shape[0]

    def raise_power():
        parts = [
            jnp.dot(power[s : s + HALF, :], power[...], preferred_element_type=F32)
            for s in halves(face)
        ]
        for s, part in zip(halves(face), parts):
            power[s : s + HALF, :] = part.astype(BF16)

    def gather():
        for s in halves(face):
            rough[s : s + HALF, :] = total[s : s + HALF, :].astype(BF16)
        for s in halves(face):
            total[s : s + HALF, :] += jnp.dot(
                rough[s : s + HALF, :], power[...], preferred_element_type=F32
            )

    raise_power()
    for _ in range(3):
        gather()
        raise_power()
    gather()
    for s in halves(face):
        rough[s : s + HALF, :] = total[s : s + HALF, :].astype(BF16)
    first = jnp.zeros((8, face), F32)
    for s in halves(face):
        part = jnp.dot(
            k_left[s : s + HALF, 0:face], rough[...], preferred_element_type=F32
        ) + jnp.dot(
            k_left[s : s + HALF, 2 * face : 3 * face], rough[...], preferred_element_type=F32
        )
        part = part - rough[s : s + HALF, :].astype(F32) + eye_rows(s, face)
        spare[s : s + HALF, :] = part
        power[s : s + HALF, :] = part.astype(BF16)
        first += chunk_sum(part * part)
    second = jnp.zeros((8, face), F32)
    for s in halves(face):
        part = jnp.dot(power[s : s + HALF, :], power[...], preferred_element_type=F32)
        second += chunk_sum(part * part)
        spare[s : s + HALF, :] += part
    for s in halves(face):
        power[s : s + HALF, :] = spare[s : s + HALF, :].astype(BF16)
    for s in halves(face):
        total[s : s + HALF, :] = rough[s : s + HALF, :].astype(F32) + jnp.dot(
            rough[s : s + HALF, :], power[...], preferred_element_type=F32
        )
    first, second = jnp.sum(first), jnp.sum(second)

    @pl.when(jnp.logical_not((first < 0.25) & (first * second < FINE)))
    def _():
        careful(k_left, total, left, right, spare)


def careful(k_left, total, left, right, spare):
    face = total.shape[0]
    for s in halves(face):
        kept = k_left[s : s + HALF, 0:face].astype(F32)
        kept += k_left[s : s + HALF, 2 * face : 3 * face].astype(F32)
        spare[s : s + HALF, :] = kept
        total[s : s + HALF, :] = kept + eye_rows(s, face)

    def raise_power():
        fill(put_left, left, spare)
        fill(put_right, right, spare)
        size = 0.0
        for s in halves(face):
            part = product(left, right, s)
            spare[s : s + HALF, :] = part
            size += jnp.sum(part * part)
        return size

    def squaring(state):
        count, _ = state
        fill(put_left, left, total)
        fill(put_right, right, spare)
        for s in halves(face):
            total[s : s + HALF, :] += product(left, right, s)
        return count + 1, raise_power()

    lax.while_loop(
        lambda state: (state[1] > 1e-15) & (state[0] < 48),
        squaring,
        (jnp.int32(0), raise_power()),
    )

    def newton(state):
        count, last, _ = state
        fill(put_right, right, total)
        size = 0.0
        for s in halves(face):
            part = product(k_left, right, s) - total[s : s + HALF, :] + eye_rows(s, face)
            spare[s : s + HALF, :] = part
            size += jnp.sum(part * part)
        better = size < 0.25 * last

        @pl.when(better)
        def _():
            fill(put_left, left, total)
            fill(put_right, right, spare)
            for s in halves(face):
                total[s : s + HALF, :] += product(left, right, s)

        return count + 1, size, better

    lax.while_loop(
        lambda state: state[2] & (state[0] < 4),
        newton,
        (jnp.int32(0), jnp.float32(1.0), jnp.bool_(True)),
    )


def fetcher(maps, sems, face):
    def fetch(slot, leaf, row, col, dst):
        copy = pltpu.make_async_copy(
            maps.at[
                0,
                leaf,
                pl.ds(pl.multiple_of(row * face, face), face),
                pl.ds(pl.multiple_of(col * face, face), face),
            ],
            dst,
            sems.at[slot],
        )
        copy.start()
        return copy

    return fetch


def started(src, dst, sem):
    copy = pltpu.make_async_copy(src, dst, sem)
    copy.start()
    return copy


def cas_rows(mode_ids, planes, shape):
    here = lax.axis_index("gz")
    core = here % 2
    row = lax.broadcasted_iota(jnp.int32, shape, 0)
    col = lax.broadcasted_iota(jnp.int32, shape, 1)
    mode = jnp.zeros(shape, jnp.int32)
    for slot in range(shape[0]):
        mode = jnp.where(row == slot, mode_ids[2 * slot + core], mode)
    start = jnp.where(col < planes, here * planes, (here - 2 * core) * planes)
    phase = mode * (start + col) & (NZ - 1)
    quarter = (phase + NZ // 8) // (NZ // 4)
    angle = (phase - quarter * (NZ // 4)).astype(F32) * (2.0 * jnp.pi / NZ)
    power = angle * angle
    cosine = jnp.ones(shape, F32)
    sine = jnp.ones(shape, F32)
    for k in (5, 4, 3, 2, 1):
        cosine = 1.0 - power * cosine * (1.0 / ((2 * k - 1) * (2 * k)))
        sine = 1.0 - power * sine * (1.0 / ((2 * k) * (2 * k + 1)))
    sine = sine * angle
    value = jnp.where(quarter % 2 == 0, cosine + sine, cosine - sine)
    return jnp.where(quarter % 4 < 2, value, -value) * (1.0 / NZ**0.5)


def near_kernel(maps, o_33_out, o_31_out, gain_out, inv_out, through_out, *scratch):
    a_33, b_33, b_32, b_23, b_22, a_31, gain, inv, through = scratch[:9]
    l_one, l_two, k_left, r_one, r_two, power, rough, spare, sems = scratch[9:]
    face = a_33.shape[0]
    far = lax.axis_index("box") % 2
    near = 1 - far
    fetch = fetcher(maps, sems, face)
    copies = [
        fetch(0, far, near, near, a_33),
        fetch(1, near, far, far, b_33),
    ]
    copies[0].wait()
    fill(put_left, l_one, a_33)
    copies[1].wait()
    copies += [
        fetch(2, near, far, near, b_32),
        fetch(3, near, near, far, b_23),
        fetch(4, near, near, near, b_22),
        fetch(5, far, near, far, a_31),
    ]
    fill(put_right, r_one, b_33)
    for s in halves(face):
        part = product(l_one, r_one, s)
        put_left(k_left, s, part)
        power[s : s + HALF, :] = part.astype(BF16)
        inv[s : s + HALF, :] = part + eye_rows(s, face)
    copies[2].wait()
    fill(put_right, r_one, b_32)
    for s in halves(face):
        part = product(l_one, r_one, s)
        through[s : s + HALF, :] = part
        put_right(r_two, s, part)
    outs = [started(through, through_out, sems.at[6])]
    invert(k_left, inv, power, rough, l_one, r_one, spare)
    outs.append(started(inv, inv_out, sems.at[7]))
    copies[3].wait()
    fill(put_left, l_one, b_23)
    fill(put_right, r_one, inv)
    for s in halves(face):
        part = product(l_one, r_one, s)
        gain[s : s + HALF, :] = part
        put_left(l_two, s, part)
    outs.append(started(gain, gain_out, sems.at[8]))
    copies[4].wait()
    for s in halves(face):
        rows = slice(s, s + HALF)
        b_22[rows, :] += product(l_two, r_two, s)
        outs.append(started(b_22.at[rows, :], o_33_out.at[rows, :], sems.at[9 + s // HALF]))
    copies[5].wait()
    fill(put_right, r_one, a_31)
    for s in halves(face):
        rows = slice(s, s + HALF)
        a_31[rows, :] = -product(l_two, r_one, s)
        outs.append(started(a_31.at[rows, :], o_31_out.at[rows, :], sems.at[11 + s // HALF]))
    for copy in outs:
        copy.wait()


def keep_pair(highs, lows, start, value):
    high, low = split(value)
    highs[start : start + value.shape[0], :] = high
    lows[start : start + value.shape[0], :] = low


def rows_times(rows, highs, lows):
    r_high, r_low = split(rows)

    def dot(left, right):
        return lax.dot_general(
            left, right, (((1,), (1,)), ((), ())), preferred_element_type=F32
        )

    return dot(r_high, highs[...]) + (dot(r_low, highs[...]) + dot(r_high, lows[...]))


def top_kernel(y_33, o_33, o_31_in, o_13_in, o_11_in, out, gain_out, *scratch):
    o_31, o_13, o_11, gain, inv = scratch[:5]
    l_one, k_left, r_one, r_two, power, rough, spare, sems = scratch[5:]
    face = y_33.shape[0]
    far = lax.axis_index("box") % 2
    copies = [
        started(src, dst, sems.at[slot])
        for slot, (src, dst) in enumerate(((o_31_in, o_31), (o_13_in, o_13), (o_11_in, o_11)))
    ]
    fill(put_left, l_one, y_33)
    fill(put_right, r_one, o_33)
    for s in halves(face):
        part = product(l_one, r_one, s)
        put_left(k_left, s, part)
        power[s : s + HALF, :] = part.astype(BF16)
        inv[s : s + HALF, :] = part + eye_rows(s, face)
    copies[0].wait()
    fill(put_right, r_one, o_31)
    for s in halves(face):
        put_right(r_two, s, product(l_one, r_one, s))
    invert(k_left, inv, power, rough, l_one, r_one, spare)
    copies[1].wait()
    fill(put_left, l_one, o_13)
    fill(put_right, r_one, inv)
    for s in halves(face):
        part = product(l_one, r_one, s)
        gain[s : s + HALF, :] = part
        put_left(k_left, s, part)
    last = [started(gain, gain_out, sems.at[5])]
    scale = (2.0 * face) ** 0.5
    copies[2].wait()
    for s in halves(face):
        o_11[s : s + HALF, :] = (o_11[s : s + HALF, :] + product(k_left, r_two, s)) * scale
        last.append(
            started(
                o_11.at[s : s + HALF, :],
                out.at[s : s + HALF, pl.ds(pl.multiple_of(far * face, face), face)],
                sems.at[6 + s // HALF],
            )
        )
    for copy in last:
        copy.wait()


def last_kernel(
    y_32, gain, y_33, near_data, far_data, other_data, _, out, data, other, left, right, sems
):
    face = gain.shape[0]
    near = 1 - lax.axis_index("box") % 2
    scale = (2.0 * face) ** 0.5
    fill(put_left, left, gain)
    fill(put_right, right, y_32)
    copies = []
    for s in halves(face):
        other[s : s + HALF, :] = product(left, right, s) * -scale
        copies.append(
            started(
                other.at[s : s + HALF, :],
                out.at[s : s + HALF, pl.ds(pl.multiple_of(near * face, face), face)],
                sems.at[s // HALF],
            )
        )
    jump = rows_times(near_data[...], *split(y_33[...])) - other_data[...]
    data[...] = far_data[...] + rows_times(jump, *split(gain[...]))
    for copy in copies:
        copy.wait()


def sums_kernel(
    mode_ids, own_in, other_in, maps, inv_in, through_in, near_gain_in, o_11_out, o_13_out, *scratch
):
    near_data, far_data, sent, got, mine, side_sent, side_got, send_sem, recv_sem = scratch[:9]
    a_13, b_33, b_32, a_11, a_31, a_33, inv, through, near_gain, gain, o_13 = scratch[9:20]
    left, r_one, r_two, near_high, near_low, far_high, far_low, own, other, cas_made, cas, sems = scratch[20:]
    face = inv.shape[0]
    far = lax.axis_index("box") % 2
    near = 1 - far
    fetch = fetcher(maps, sems, face)
    planes_in = (started(own_in, own, sems.at[11]), started(other_in, other, sems.at[12]))
    here = lax.axis_index("gz")
    core, z, x = here % 2, here // 2 % 8, here // 16

    def device(x_at, z_at):
        return {"gz": x_at * 16 + z_at * 2 + core}

    ring = (device(x, (z + 1) % 8), device(x, (z + 7) % 8))
    beside = device(1 - x, z)
    barrier = pltpu.get_barrier_semaphore()
    for target in (*ring, beside):
        pl.semaphore_signal(barrier, inc=1, device_id=target, device_id_type=MESH)
    cas_made[...] = cas_rows(mode_ids, own.shape[0], cas_made.shape)
    cas_in = started(cas_made, cas, sems.at[13])
    for copy in planes_in:
        copy.wait()
    cas_in.wait()
    copies_in = [
        fetch(0, far, far, near, a_13),
        fetch(1, near, far, far, b_33),
        fetch(2, near, far, near, b_32),
        started(inv_in, inv, sems.at[3]),
        fetch(4, far, near, far, a_31),
        fetch(5, far, far, far, a_11),
        started(through_in, through, sems.at[6]),
        fetch(7, far, near, near, a_33),
        started(near_gain_in, near_gain, sems.at[8]),
    ]
    planes = own.shape[0]

    def term(x_to, z_to, store):
        row = x_to * 8 + z_to

        def block(part, carry):
            rows = pl.ds(pl.multiple_of(part * 8, 8), 8)
            total = cas[row, 0] * own[0, rows, :]
            for k in range(1, planes):
                total += cas[row, k] * own[k, rows, :]
            for k in range(planes):
                total += cas[row, planes + k] * other[k, rows, :]
            store(rows, total)
            return carry

        lax.fori_loop(0, own.shape[1] // 8, block, 0)

    def message(way, index):
        return pltpu.make_async_remote_copy(
            src_ref=sent.at[way, index],
            dst_ref=got.at[way, index],
            send_sem=send_sem.at[way, index],
            recv_sem=recv_sem.at[way, index],
            device_id=ring[way],
            device_id_type=MESH,
        )

    copies_out = []

    def work_0():
        copies_in[0].wait()
        fill(put_left, left, a_13)
        copies_in[1].wait()
        fill(put_right, r_one, b_33)
        for s in halves(face):
            gain[s : s + HALF, :] = product(left, r_one, s)

    def work_1():
        copies_in[2].wait()
        fill(put_right, r_two, b_32)
        for s in halves(face):
            o_13[s : s + HALF, :] = -product(left, r_two, s)

    def work_2():
        copies_in[3].wait()
        fill(put_left, left, gain)
        fill(put_right, r_one, inv)
        for s in halves(face):
            gain[s : s + HALF, :] = product(left, r_one, s)

    def work_3():
        fill(put_left, left, gain)
        copies_in[4].wait()
        copies_in[5].wait()
        fill(put_right, r_one, a_31)
        for s in halves(face):
            a_11[s : s + HALF, :] += product(left, r_one, s)
        copies_out.append(started(a_11, o_11_out, sems.at[9]))

    def work_4():
        copies_in[6].wait()
        fill(put_right, r_two, through)
        for s in halves(face):
            o_13[s : s + HALF, :] -= product(left, r_two, s)
        copies_out.append(started(o_13, o_13_out, sems.at[10]))

    def work_5():
        copies_in[7].wait()
        copies_in[8].wait()
        for s in halves(face):
            rows = slice(s, s + HALF)
            keep_pair(far_high, far_low, s, a_33[rows, :])
            keep_pair(far_high, far_low, face + s, a_13[rows, :])
            keep_pair(near_high, near_low, s, near_gain[rows, :])
            keep_pair(near_high, near_low, face + s, gain[rows, :])

    work = (work_0, work_1, work_2, work_3, work_4, work_5, lambda: None)
    copies = [[message(way, index) for index in range(7)] for way in range(2)]
    for index in range(7):
        step = (index + 3) // 2
        first = index % 2 == 0
        for way in range(2):
            x_to = way if first else 1 - way
            z_to = (z + (5 - step)) % 8 if way == 0 else (z + 8 - (5 - step)) % 8

            def store(rows, total, way=way, index=index):
                sent[way, index, rows, :] = total

            term(x_to, z_to, store)
            if index == 0 and way == 0:
                pl.semaphore_wait(barrier, 3)
            if index >= 2:
                copies[way][index - 2].wait_recv()
                sent[way, index] += got[way, index - 2]
            copies[way][index].start()
        work[index]()
    for x_to in range(2):

        def store(rows, total, x_to=x_to):
            mine[x_to, rows, :] = total

        term(x_to, z, store)
    for index in (5, 6):
        for way in range(2):
            copies[way][index].wait_recv()
    away = 1 - x
    side_sent[...] = mine[away] + (got[0, 6 - away] + got[1, 5 + away])
    last = pltpu.make_async_remote_copy(
        src_ref=side_sent,
        dst_ref=side_got,
        send_sem=send_sem.at[2, 0],
        recv_sem=recv_sem.at[2, 0],
        device_id=beside,
        device_id_type=MESH,
    )
    last.start()
    mine[x] += got[0, 6 - x] + got[1, 5 + x]
    last.wait_recv()
    mine[x] += side_got[...]
    rhs = near_data.shape[0]

    def info(leaf, side):
        return mine[
            x,
            pl.ds(pl.multiple_of(leaf * rhs, rhs), rhs),
            pl.ds(pl.multiple_of(side * face, face), face),
        ]

    known = rows_times(info(near, far), far_high, far_low)
    jump = info(far, near) - known[:, 0:face]
    moved = rows_times(jump, near_high, near_low)
    near_data[...] = info(near, near) - moved[:, 0:face]
    far_data[...] = info(far, far) + moved[:, face : 2 * face] - known[:, face : 2 * face]
    for way in range(2):
        for index in range(7):
            copies[way][index].wait_send()
    last.wait_send()
    for copy in copies_out:
        copy.wait()


def vmem_specs(count):
    return [pl.BlockSpec(memory_space=pltpu.VMEM)] * count


ANY = pl.BlockSpec(memory_space=pl.ANY)


def local(sources, leaf_maps, mode_ids):
    planes, boxes, rhs, points = sources.shape
    face = points // 2
    square = jax.ShapeDtypeStruct((face, face), F32)
    rows = jax.ShapeDtypeStruct((rhs, face), F32)
    full = pltpu.VMEM((face, face), F32)
    short = pltpu.VMEM((face, face), BF16)
    left = pltpu.VMEM((face, 3 * face), BF16)
    right = pltpu.VMEM((3 * face, face), BF16)
    params = pltpu.CompilerParams(vmem_limit_bytes=VMEM_LIMIT)

    def cost(units, size):
        return pl.CostEstimate(
            flops=units * 2 * face**3, bytes_accessed=size * 4 * face**2, transcendentals=0
        )

    other_sources = swapped(sources, "gz")
    o_33, o_31, near_gain, inv, through = pl.pallas_call(
        near_kernel,
        out_shape=[square] * 5,
        in_specs=[ANY],
        out_specs=[ANY] * 5,
        scratch_shapes=[full] * 9
        + [left, left, left, right, right, short, short, full, pltpu.SemaphoreType.DMA((13,))],
        compiler_params=params,
        cost_estimate=cost(27, 11),
        name="level_one_near",
    )(leaf_maps)
    y_33 = swapped(o_33, "box")
    y_32 = swapped(o_31, "box")
    line = (boxes * rhs, points)
    pair = pltpu.VMEM((2 * face, face), BF16)
    o_11, o_13, near_data, far_data = pl.pallas_call(
        sums_kernel,
        out_shape=[square, square, rows, rows],
        in_specs=[pl.BlockSpec(memory_space=pltpu.SMEM)] + [ANY] * 6,
        out_specs=[ANY] * 2 + vmem_specs(2),
        scratch_shapes=[
            pltpu.VMEM((2, 7, *line), F32),
            pltpu.VMEM((2, 7, *line), F32),
            pltpu.VMEM((2, *line), F32),
            pltpu.VMEM(line, F32),
            pltpu.VMEM(line, F32),
            pltpu.SemaphoreType.DMA((3, 7)),
            pltpu.SemaphoreType.DMA((3, 7)),
        ]
        + [full] * 11
        + [left, right, right, pair, pair, pair, pair]
        + [pltpu.VMEM((planes, *line), F32)] * 2
        + [space((mode_ids.shape[0] // 2, 128), F32) for space in (pltpu.VMEM, pltpu.SMEM)]
        + [pltpu.SemaphoreType.DMA((14,))],
        compiler_params=pltpu.CompilerParams(
            vmem_limit_bytes=VMEM_LIMIT, collective_id=0, has_side_effects=True
        ),
        cost_estimate=cost(100, 5),
        name="hartley_sums",
    )(
        mode_ids,
        sources.reshape(planes, *line),
        other_sources.reshape(planes, *line),
        leaf_maps,
        inv,
        through,
        near_gain,
    )
    other_data = swapped(near_data, "box")
    out, gain = pl.pallas_call(
        top_kernel,
        out_shape=[jax.ShapeDtypeStruct((face, points), F32), square],
        in_specs=vmem_specs(2) + [ANY] * 3,
        out_specs=[ANY] * 2,
        scratch_shapes=[full] * 5
        + [left, left, right, right, short, short, full, pltpu.SemaphoreType.DMA((8,))],
        compiler_params=pltpu.CompilerParams(vmem_limit_bytes=LESS_VMEM),
        cost_estimate=cost(22, 8),
        name="level_two_gain",
    )(y_33, o_33, o_31, o_13, o_11)
    out, data = pl.pallas_call(
        last_kernel,
        out_shape=[jax.ShapeDtypeStruct((face, points), F32), rows],
        in_specs=vmem_specs(6) + [ANY],
        out_specs=[ANY] + vmem_specs(1),
        scratch_shapes=[full, left, right, pltpu.SemaphoreType.DMA((2,))],
        input_output_aliases={6: 0},
        compiler_params=pltpu.CompilerParams(vmem_limit_bytes=LAST_VMEM),
        cost_estimate=cost(4, 5),
        name="level_two_rows",
    )(y_32, gain, y_33, near_data, far_data, other_data, out)
    return (out[None, None], data[None, None])


def solution(mesh):
    placed = (P("gz", "box", None, None), P("gz", "box", None, None), P())
    return jax.shard_map(
        local,
        mesh=mesh,
        in_specs=placed,
        out_specs=(P("gz", "box", None, None), P("gz", "box", None, None)),
        check_vma=False,
    )
```

```python
import jax
import jax.numpy as jnp
from jax import lax
from jax.experimental import pallas as pl
from jax.experimental.pallas import tpu as pltpu
from jax.sharding import PartitionSpec as P

NZ = 512
MESH = pl.DeviceIdType.MESH
F32 = jnp.float32
BF16 = jnp.bfloat16
HALF = 256
FINE = 3.6e-9
VMEM_LIMIT = 60 * 1024 * 1024
LESS_VMEM = 50 * 1024 * 1024
LAST_VMEM = 28 * 1024 * 1024


def swapped(block, axis):
    count = lax.axis_size(axis)
    route = []
    for low in range(0, count, 2):
        route += [(low, low + 1), (low + 1, low)]
    return lax.ppermute(block, axis, route)


def split(value):
    high = value.astype(BF16)
    return high, (value - high.astype(F32)).astype(BF16)


def put_left(ref, start, value):
    face = value.shape[1]
    high, low = split(value)
    rows = pl.ds(start, value.shape[0])
    ref[rows, 0:face] = high
    ref[rows, face : 2 * face] = high
    ref[rows, 2 * face : 3 * face] = low


def put_right(ref, start, value):
    face = ref.shape[0] // 3
    high, low = split(value)
    count = value.shape[0]
    ref[pl.ds(start, count), :] = high
    ref[pl.ds(face + start, count), :] = low
    ref[pl.ds(2 * face + start, count), :] = high


def fill(put, ref, source):
    for start in range(0, source.shape[0], HALF):
        put(ref, start, source[start : start + HALF, :])


def product(left, right, start):
    return jnp.dot(left[start : start + HALF, :], right[...], preferred_element_type=F32)


def halves(face):
    return range(0, face, HALF)


def eye_rows(start, face):
    row = lax.broadcasted_iota(jnp.int32, (HALF, face), 0) + start
    col = lax.broadcasted_iota(jnp.int32, (HALF, face), 1)
    return jnp.where(row == col, 1.0, 0.0).astype(F32)


def chunk_sum(part):
    return jnp.sum(part.reshape(-1, 8, part.shape[1]), axis=0)


def invert(k_left, total, power, rough, left, right, spare):
    face = total.shape[0]

    def raise_power():
        parts = [
            jnp.dot(power[s : s + HALF, :], power[...], preferred_element_type=F32)
            for s in halves(face)
        ]
        for s, part in zip(halves(face), parts):
            power[s : s + HALF, :] = part.astype(BF16)

    def gather():
        for s in halves(face):
            rough[s : s + HALF, :] = total[s : s + HALF, :].astype(BF16)
        for s in halves(face):
            total[s : s + HALF, :] += jnp.dot(
                rough[s : s + HALF, :], power[...], preferred_element_type=F32
            )

    raise_power()
    for _ in range(3):
        gather()
        raise_power()
    gather()
    for s in halves(face):
        rough[s : s + HALF, :] = total[s : s + HALF, :].astype(BF16)
    first = jnp.zeros((8, face), F32)
    for s in halves(face):
        part = jnp.dot(
            k_left[s : s + HALF, 0:face], rough[...], preferred_element_type=F32
        ) + jnp.dot(
            k_left[s : s + HALF, 2 * face : 3 * face], rough[...], preferred_element_type=F32
        )
        part = part - rough[s : s + HALF, :].astype(F32) + eye_rows(s, face)
        spare[s : s + HALF, :] = part
        power[s : s + HALF, :] = part.astype(BF16)
        first += chunk_sum(part * part)
    second = jnp.zeros((8, face), F32)
    for s in halves(face):
        part = jnp.dot(power[s : s + HALF, :], power[...], preferred_element_type=F32)
        second += chunk_sum(part * part)
        spare[s : s + HALF, :] += part
    for s in halves(face):
        power[s : s + HALF, :] = spare[s : s + HALF, :].astype(BF16)
    for s in halves(face):
        total[s : s + HALF, :] = rough[s : s + HALF, :].astype(F32) + jnp.dot(
            rough[s : s + HALF, :], power[...], preferred_element_type=F32
        )
    first, second = jnp.sum(first), jnp.sum(second)

    @pl.when(jnp.logical_not((first < 0.25) & (first * second < FINE)))
    def _():
        careful(k_left, total, left, right, spare)


def careful(k_left, total, left, right, spare):
    face = total.shape[0]
    for s in halves(face):
        kept = k_left[s : s + HALF, 0:face].astype(F32)
        kept += k_left[s : s + HALF, 2 * face : 3 * face].astype(F32)
        spare[s : s + HALF, :] = kept
        total[s : s + HALF, :] = kept + eye_rows(s, face)

    def raise_power():
        fill(put_left, left, spare)
        fill(put_right, right, spare)
        size = 0.0
        for s in halves(face):
            part = product(left, right, s)
            spare[s : s + HALF, :] = part
            size += jnp.sum(part * part)
        return size

    def squaring(state):
        count, _ = state
        fill(put_left, left, total)
        fill(put_right, right, spare)
        for s in halves(face):
            total[s : s + HALF, :] += product(left, right, s)
        return count + 1, raise_power()

    lax.while_loop(
        lambda state: (state[1] > 1e-15) & (state[0] < 48),
        squaring,
        (jnp.int32(0), raise_power()),
    )

    def newton(state):
        count, last, _ = state
        fill(put_right, right, total)
        size = 0.0
        for s in halves(face):
            part = product(k_left, right, s) - total[s : s + HALF, :] + eye_rows(s, face)
            spare[s : s + HALF, :] = part
            size += jnp.sum(part * part)
        better = size < 0.25 * last

        @pl.when(better)
        def _():
            fill(put_left, left, total)
            fill(put_right, right, spare)
            for s in halves(face):
                total[s : s + HALF, :] += product(left, right, s)

        return count + 1, size, better

    lax.while_loop(
        lambda state: state[2] & (state[0] < 4),
        newton,
        (jnp.int32(0), jnp.float32(1.0), jnp.bool_(True)),
    )


def fetcher(maps, sems, face):
    def fetch(slot, leaf, row, col, dst):
        copy = pltpu.make_async_copy(
            maps.at[
                0,
                leaf,
                pl.ds(pl.multiple_of(row * face, face), face),
                pl.ds(pl.multiple_of(col * face, face), face),
            ],
            dst,
            sems.at[slot],
        )
        copy.start()
        return copy

    return fetch


def started(src, dst, sem):
    copy = pltpu.make_async_copy(src, dst, sem)
    copy.start()
    return copy


def cas_rows(mode_ids, planes, shape):
    here = lax.axis_index("gz")
    core = here % 2
    row = lax.broadcasted_iota(jnp.int32, shape, 0)
    col = lax.broadcasted_iota(jnp.int32, shape, 1)
    mode = jnp.zeros(shape, jnp.int32)
    for slot in range(shape[0]):
        mode = jnp.where(row == slot, mode_ids[2 * slot + core], mode)
    start = jnp.where(col < planes, here * planes, (here - 2 * core) * planes)
    phase = mode * (start + col) & (NZ - 1)
    quarter = (phase + NZ // 8) // (NZ // 4)
    angle = (phase - quarter * (NZ // 4)).astype(F32) * (2.0 * jnp.pi / NZ)
    power = angle * angle
    cosine = jnp.ones(shape, F32)
    sine = jnp.ones(shape, F32)
    for k in (5, 4, 3, 2, 1):
        cosine = 1.0 - power * cosine * (1.0 / ((2 * k - 1) * (2 * k)))
        sine = 1.0 - power * sine * (1.0 / ((2 * k) * (2 * k + 1)))
    sine = sine * angle
    value = jnp.where(quarter % 2 == 0, cosine + sine, cosine - sine)
    return jnp.where(quarter % 4 < 2, value, -value) * (1.0 / NZ**0.5)


def near_kernel(maps, o_33_out, o_31_out, gain_out, inv_out, through_out, *scratch):
    a_33, b_33, b_32, b_23, b_22, a_31, gain, inv, through = scratch[:9]
    l_one, l_two, k_left, r_one, r_two, power, rough, spare, sems = scratch[9:]
    face = a_33.shape[0]
    far = lax.axis_index("box") % 2
    near = 1 - far
    fetch = fetcher(maps, sems, face)
    copies = [
        fetch(0, far, near, near, a_33),
        fetch(1, near, far, far, b_33),
    ]
    copies[0].wait()
    fill(put_left, l_one, a_33)
    copies[1].wait()
    copies += [
        fetch(2, near, far, near, b_32),
        fetch(3, near, near, far, b_23),
        fetch(4, near, near, near, b_22),
        fetch(5, far, near, far, a_31),
    ]
    fill(put_right, r_one, b_33)
    for s in halves(face):
        part = product(l_one, r_one, s)
        put_left(k_left, s, part)
        power[s : s + HALF, :] = part.astype(BF16)
        inv[s : s + HALF, :] = part + eye_rows(s, face)
    copies[2].wait()
    fill(put_right, r_one, b_32)
    for s in halves(face):
        part = product(l_one, r_one, s)
        through[s : s + HALF, :] = part
        put_right(r_two, s, part)
    outs = [started(through, through_out, sems.at[6])]
    invert(k_left, inv, power, rough, l_one, r_one, spare)
    outs.append(started(inv, inv_out, sems.at[7]))
    copies[3].wait()
    fill(put_left, l_one, b_23)
    fill(put_right, r_one, inv)
    for s in halves(face):
        part = product(l_one, r_one, s)
        gain[s : s + HALF, :] = part
        put_left(l_two, s, part)
    outs.append(started(gain, gain_out, sems.at[8]))
    copies[4].wait()
    for s in halves(face):
        rows = slice(s, s + HALF)
        b_22[rows, :] += product(l_two, r_two, s)
        outs.append(started(b_22.at[rows, :], o_33_out.at[rows, :], sems.at[9 + s // HALF]))
    copies[5].wait()
    fill(put_right, r_one, a_31)
    for s in halves(face):
        rows = slice(s, s + HALF)
        a_31[rows, :] = -product(l_two, r_one, s)
        outs.append(started(a_31.at[rows, :], o_31_out.at[rows, :], sems.at[11 + s // HALF]))
    for copy in outs:
        copy.wait()


def keep_pair(highs, lows, start, value):
    high, low = split(value)
    highs[start : start + value.shape[0], :] = high
    lows[start : start + value.shape[0], :] = low


def rows_times(rows, highs, lows):
    r_high, r_low = split(rows)

    def dot(left, right):
        return lax.dot_general(
            left, right, (((1,), (1,)), ((), ())), preferred_element_type=F32
        )

    return dot(r_high, highs[...]) + (dot(r_low, highs[...]) + dot(r_high, lows[...]))


def top_kernel(
    y_33, o_33, o_31_in, o_13_in, o_11_in, near_in, out, gain_out, mirrored, *scratch
):
    o_31, o_13, o_11, gain, inv = scratch[:5]
    l_one, k_left, r_one, r_two, power, rough, spare, near_data, sems = scratch[5:]
    face = y_33.shape[0]
    far = lax.axis_index("box") % 2
    copies = [
        started(src, dst, sems.at[slot])
        for slot, (src, dst) in enumerate(((o_31_in, o_31), (o_13_in, o_13), (o_11_in, o_11)))
    ]
    news = started(near_in, near_data, sems.at[8])
    fill(put_left, l_one, y_33)
    fill(put_right, r_one, o_33)
    for s in halves(face):
        part = product(l_one, r_one, s)
        put_left(k_left, s, part)
        power[s : s + HALF, :] = part.astype(BF16)
        inv[s : s + HALF, :] = part + eye_rows(s, face)
    copies[0].wait()
    fill(put_right, r_one, o_31)
    for s in halves(face):
        put_right(r_two, s, product(l_one, r_one, s))
    news.wait()
    mirrored[...] = rows_times(near_data[...], l_one.at[:, 0:face], l_one.at[:, 2 * face :])
    invert(k_left, inv, power, rough, l_one, r_one, spare)
    copies[1].wait()
    fill(put_left, l_one, o_13)
    fill(put_right, r_one, inv)
    for s in halves(face):
        part = product(l_one, r_one, s)
        gain[s : s + HALF, :] = part
        put_left(k_left, s, part)
    last = [started(gain, gain_out, sems.at[5])]
    scale = (2.0 * face) ** 0.5
    copies[2].wait()
    for s in halves(face):
        o_11[s : s + HALF, :] = (o_11[s : s + HALF, :] + product(k_left, r_two, s)) * scale
        last.append(
            started(
                o_11.at[s : s + HALF, :],
                out.at[s : s + HALF, pl.ds(pl.multiple_of(far * face, face), face)],
                sems.at[6 + s // HALF],
            )
        )
    for copy in last:
        copy.wait()


def last_kernel(
    y_32, gain, mirrored, far_data, other_data, _, out, data, other, left, right, sems
):
    face = gain.shape[0]
    near = 1 - lax.axis_index("box") % 2
    scale = (2.0 * face) ** 0.5
    fill(put_left, left, gain)
    fill(put_right, right, y_32)
    copies = []
    for s in halves(face):
        other[s : s + HALF, :] = product(left, right, s) * -scale
        copies.append(
            started(
                other.at[s : s + HALF, :],
                out.at[s : s + HALF, pl.ds(pl.multiple_of(near * face, face), face)],
                sems.at[s // HALF],
            )
        )
    jump = mirrored[...] - other_data[...]
    data[...] = far_data[...] + rows_times(jump, left.at[:, 0:face], left.at[:, 2 * face :])
    for copy in copies:
        copy.wait()


def sums_kernel(
    mode_ids, own_in, other_in, maps, inv_in, through_in, near_gain_in, o_11_out, o_13_out, *scratch
):
    near_data, far_data, sent, got, mine, side_sent, side_got, send_sem, recv_sem = scratch[:9]
    a_13, b_33, b_32, a_11, a_31, a_33, inv, through, near_gain, gain, o_13 = scratch[9:20]
    left, r_one, r_two, near_high, near_low, far_high, far_low, own, other, cas_made, cas, sems = scratch[20:]
    face = inv.shape[0]
    far = lax.axis_index("box") % 2
    near = 1 - far
    fetch = fetcher(maps, sems, face)
    planes_in = (started(own_in, own, sems.at[11]), started(other_in, other, sems.at[12]))
    here = lax.axis_index("gz")
    core, z, x = here % 2, here // 2 % 8, here // 16

    def device(x_at, z_at):
        return {"gz": x_at * 16 + z_at * 2 + core}

    ring = (device(x, (z + 1) % 8), device(x, (z + 7) % 8))
    beside = device(1 - x, z)
    barrier = pltpu.get_barrier_semaphore()
    for target in (*ring, beside):
        pl.semaphore_signal(barrier, inc=1, device_id=target, device_id_type=MESH)
    cas_made[...] = cas_rows(mode_ids, own.shape[0], cas_made.shape)
    cas_in = started(cas_made, cas, sems.at[13])
    for copy in planes_in:
        copy.wait()
    cas_in.wait()
    copies_in = [
        fetch(0, far, far, near, a_13),
        fetch(1, near, far, far, b_33),
        fetch(2, near, far, near, b_32),
        started(inv_in, inv, sems.at[3]),
        fetch(4, far, near, far, a_31),
        fetch(5, far, far, far, a_11),
        started(through_in, through, sems.at[6]),
        fetch(7, far, near, near, a_33),
        started(near_gain_in, near_gain, sems.at[8]),
    ]
    planes = own.shape[0]

    def term(x_to, z_to, store):
        row = x_to * 8 + z_to

        def block(part, carry):
            rows = pl.ds(pl.multiple_of(part * 8, 8), 8)
            total = cas[row, 0] * own[0, rows, :]
            for k in range(1, planes):
                total += cas[row, k] * own[k, rows, :]
            for k in range(planes):
                total += cas[row, planes + k] * other[k, rows, :]
            store(rows, total)
            return carry

        lax.fori_loop(0, own.shape[1] // 8, block, 0)

    def message(way, index):
        return pltpu.make_async_remote_copy(
            src_ref=sent.at[way, index],
            dst_ref=got.at[way, index],
            send_sem=send_sem.at[way, index],
            recv_sem=recv_sem.at[way, index],
            device_id=ring[way],
            device_id_type=MESH,
        )

    copies_out = []

    def work_0():
        copies_in[0].wait()
        fill(put_left, left, a_13)
        copies_in[1].wait()
        fill(put_right, r_one, b_33)
        for s in halves(face):
            gain[s : s + HALF, :] = product(left, r_one, s)

    def work_1():
        copies_in[2].wait()
        fill(put_right, r_two, b_32)
        for s in halves(face):
            o_13[s : s + HALF, :] = -product(left, r_two, s)

    def work_2():
        copies_in[3].wait()
        fill(put_left, left, gain)
        fill(put_right, r_one, inv)
        for s in halves(face):
            gain[s : s + HALF, :] = product(left, r_one, s)

    def work_3():
        fill(put_left, left, gain)
        copies_in[4].wait()
        copies_in[5].wait()
        fill(put_right, r_one, a_31)
        for s in halves(face):
            a_11[s : s + HALF, :] += product(left, r_one, s)
        copies_out.append(started(a_11, o_11_out, sems.at[9]))

    def work_4():
        copies_in[6].wait()
        fill(put_right, r_two, through)
        for s in halves(face):
            o_13[s : s + HALF, :] -= product(left, r_two, s)
        copies_out.append(started(o_13, o_13_out, sems.at[10]))

    def work_5():
        copies_in[7].wait()
        copies_in[8].wait()
        for s in halves(face):
            rows = slice(s, s + HALF)
            keep_pair(far_high, far_low, s, a_33[rows, :])
            keep_pair(far_high, far_low, face + s, a_13[rows, :])
            keep_pair(near_high, near_low, s, near_gain[rows, :])
            keep_pair(near_high, near_low, face + s, gain[rows, :])

    work = (work_0, work_1, work_2, work_3, work_4, work_5, lambda: None)
    copies = [[message(way, index) for index in range(7)] for way in range(2)]
    for index in range(7):
        step = (index + 3) // 2
        first = index % 2 == 0
        for way in range(2):
            x_to = way if first else 1 - way
            z_to = (z + (5 - step)) % 8 if way == 0 else (z + 8 - (5 - step)) % 8

            def store(rows, total, way=way, index=index):
                sent[way, index, rows, :] = total

            term(x_to, z_to, store)
            if index == 0 and way == 0:
                pl.semaphore_wait(barrier, 3)
            if index >= 2:
                copies[way][index - 2].wait_recv()
                sent[way, index] += got[way, index - 2]
            copies[way][index].start()
        work[index]()
    for x_to in range(2):

        def store(rows, total, x_to=x_to):
            mine[x_to, rows, :] = total

        term(x_to, z, store)
    for index in (5, 6):
        for way in range(2):
            copies[way][index].wait_recv()
    away = 1 - x
    side_sent[...] = mine[away] + (got[0, 6 - away] + got[1, 5 + away])
    last = pltpu.make_async_remote_copy(
        src_ref=side_sent,
        dst_ref=side_got,
        send_sem=send_sem.at[2, 0],
        recv_sem=recv_sem.at[2, 0],
        device_id=beside,
        device_id_type=MESH,
    )
    last.start()
    mine[x] += got[0, 6 - x] + got[1, 5 + x]
    last.wait_recv()
    mine[x] += side_got[...]
    rhs = near_data.shape[0]

    def info(leaf, side):
        return mine[
            x,
            pl.ds(pl.multiple_of(leaf * rhs, rhs), rhs),
            pl.ds(pl.multiple_of(side * face, face), face),
        ]

    known = rows_times(info(near, far), far_high, far_low)
    jump = info(far, near) - known[:, 0:face]
    moved = rows_times(jump, near_high, near_low)
    near_data[...] = info(near, near) - moved[:, 0:face]
    far_data[...] = info(far, far) + moved[:, face : 2 * face] - known[:, face : 2 * face]
    for way in range(2):
        for index in range(7):
            copies[way][index].wait_send()
    last.wait_send()
    for copy in copies_out:
        copy.wait()


def vmem_specs(count):
    return [pl.BlockSpec(memory_space=pltpu.VMEM)] * count


ANY = pl.BlockSpec(memory_space=pl.ANY)


def local(sources, leaf_maps, mode_ids):
    planes, boxes, rhs, points = sources.shape
    face = points // 2
    square = jax.ShapeDtypeStruct((face, face), F32)
    rows = jax.ShapeDtypeStruct((rhs, face), F32)
    full = pltpu.VMEM((face, face), F32)
    short = pltpu.VMEM((face, face), BF16)
    left = pltpu.VMEM((face, 3 * face), BF16)
    right = pltpu.VMEM((3 * face, face), BF16)
    params = pltpu.CompilerParams(vmem_limit_bytes=VMEM_LIMIT)

    def cost(units, size):
        return pl.CostEstimate(
            flops=units * 2 * face**3, bytes_accessed=size * 4 * face**2, transcendentals=0
        )

    other_sources = swapped(sources, "gz")
    o_33, o_31, near_gain, inv, through = pl.pallas_call(
        near_kernel,
        out_shape=[square] * 5,
        in_specs=[ANY],
        out_specs=[ANY] * 5,
        scratch_shapes=[full] * 9
        + [left, left, left, right, right, short, short, full, pltpu.SemaphoreType.DMA((13,))],
        compiler_params=params,
        cost_estimate=cost(27, 11),
        name="level_one_near",
    )(leaf_maps)
    y_33 = swapped(o_33, "box")
    y_32 = swapped(o_31, "box")
    line = (boxes * rhs, points)
    pair = pltpu.VMEM((2 * face, face), BF16)
    o_11, o_13, near_data, far_data = pl.pallas_call(
        sums_kernel,
        out_shape=[square, square, rows, rows],
        in_specs=[pl.BlockSpec(memory_space=pltpu.SMEM)] + [ANY] * 6,
        out_specs=[ANY] * 2 + vmem_specs(2),
        scratch_shapes=[
            pltpu.VMEM((2, 7, *line), F32),
            pltpu.VMEM((2, 7, *line), F32),
            pltpu.VMEM((2, *line), F32),
            pltpu.VMEM(line, F32),
            pltpu.VMEM(line, F32),
            pltpu.SemaphoreType.DMA((3, 7)),
            pltpu.SemaphoreType.DMA((3, 7)),
        ]
        + [full] * 11
        + [left, right, right, pair, pair, pair, pair]
        + [pltpu.VMEM((planes, *line), F32)] * 2
        + [space((mode_ids.shape[0] // 2, 128), F32) for space in (pltpu.VMEM, pltpu.SMEM)]
        + [pltpu.SemaphoreType.DMA((14,))],
        compiler_params=pltpu.CompilerParams(
            vmem_limit_bytes=VMEM_LIMIT, collective_id=0, has_side_effects=True
        ),
        cost_estimate=cost(100, 5),
        name="hartley_sums",
    )(
        mode_ids,
        sources.reshape(planes, *line),
        other_sources.reshape(planes, *line),
        leaf_maps,
        inv,
        through,
        near_gain,
    )
    other_data = swapped(near_data, "box")
    out, gain, mirrored = pl.pallas_call(
        top_kernel,
        out_shape=[jax.ShapeDtypeStruct((face, points), F32), square, rows],
        in_specs=vmem_specs(2) + [ANY] * 4,
        out_specs=[ANY] * 2 + vmem_specs(1),
        scratch_shapes=[full] * 5
        + [left, left, right, right, short, short, full, pltpu.VMEM((rhs, face), F32)]
        + [pltpu.SemaphoreType.DMA((9,))],
        compiler_params=pltpu.CompilerParams(vmem_limit_bytes=LESS_VMEM),
        cost_estimate=cost(22, 8),
        name="level_two_gain",
    )(y_33, o_33, o_31, o_13, o_11, near_data)
    out, data = pl.pallas_call(
        last_kernel,
        out_shape=[jax.ShapeDtypeStruct((face, points), F32), rows],
        in_specs=vmem_specs(5) + [ANY],
        out_specs=[ANY] + vmem_specs(1),
        scratch_shapes=[full, left, right, pltpu.SemaphoreType.DMA((2,))],
        input_output_aliases={5: 0},
        compiler_params=pltpu.CompilerParams(vmem_limit_bytes=LAST_VMEM),
        cost_estimate=cost(4, 5),
        name="level_two_rows",
    )(y_32, gain, mirrored, far_data, other_data, out)
    return (out[None, None], data[None, None])


def solution(mesh):
    placed = (P("gz", "box", None, None), P("gz", "box", None, None), P())
    return jax.shard_map(
        local,
        mesh=mesh,
        in_specs=placed,
        out_specs=(P("gz", "box", None, None), P("gz", "box", None, None)),
        check_vma=False,
    )
```
